32 devices in a mesh: list: 8 (over y, x, core), rep: 4 (over z).
Axes of the slice: x: 2, y: 2, z: 4, core: 2. Of those that a mesh axis runs over, the one named last changes fastest.
Arguments:
- memory_rows: bfloat16 [8192, 1024], P(('list', 'rep'))
- list_owner: int32 [8192, 1], P(('list', 'rep')), may hold values from 0 to 7; in each aligned block of 256 rows (0 to 255, 256 to 511, ...) at most 128 rows name the same one
- list_slot: int32 [8192], P(('list', 'rep')), may hold values from 0 to 2047
- pq_codes: int32 [8192, 16], P(('list', 'rep')), may hold values from 0 to 255
- valid_rows: int32 [32], P(('list', 'rep')), may hold values from 128 to 256
- centroids: bfloat16 [16384, 1024], P('list'), may hold values from -3 to 3
- codebook: float32 [16, 256, 64], replicated
Outputs:
- new_codebook: float32 [16, 256, 64], P('rep')
- row_error: float32 [8192], P(('list', 'rep'))
The draws below stay inside these ranges and needn't reach their ends.
Inputs may be any that keep to these rules, and one draw needn't show every extreme that they name: `list_owner`: the rows of one device name one index of list at most 128 times, and some device's rows name one exactly 128 times.
All inputs are finite; a program needn't handle non-finite values.
Results may differ from the reference program's by a relative error of at most 0.0038.
Values may be sent and summed in bfloat16 or wider, within the bound.
No kernel may reach another device: no remote copies, remote signals or barrier semaphores. Data moves between devices by JAX's collectives and lax.ppermute only.
A program may use at most 128 MiB of HBM per device.

```python
import math
import jax
import jax.numpy as jnp
import numpy as np
from jax import lax

D = 1024
M = 16
K = 256
DS = 64
ROWS_DEV = 256
LIST_DEV = 2048
CAP = 128
ROWS = 8192
LISTS = 16384
N_LIST = 8
DEVICES = 32


def shared_codes(key):
    uniform_codes = jax.random.randint(jax.random.fold_in(key, 11), (ROWS, M), 0, K, dtype=jnp.int32)
    offsets = jax.random.randint(jax.random.fold_in(key, 14), (M,), 0, K, dtype=jnp.int32)
    block_ids = jnp.arange(ROWS, dtype=jnp.int32) // ROWS_DEV
    favoured = (block_ids[:, None] + offsets[None, :]) % K
    pick = jax.random.randint(jax.random.fold_in(key, 15), (ROWS, M), 0, 2, dtype=jnp.int32)
    return jnp.where(pick == 1, favoured, uniform_codes).astype(jnp.int32)


def shared_book(key):
    return jax.random.normal(jax.random.fold_in(key, 12), (M, K, DS), jnp.float32)


def draw_pq_codes(key, part):
    return shared_codes(key)


def draw_codebook(key, part):
    return shared_book(key)


def draw_memory_rows(key, part):
    codes_drawn = shared_codes(key)
    book = shared_book(key)
    recon = book[jnp.arange(M)[None, :], codes_drawn].reshape(ROWS, D)
    noise_key = jax.random.fold_in(key, 13)
    block_bias = jax.random.normal(jax.random.fold_in(key, 16), (ROWS // ROWS_DEV, D), jnp.float32)
    bias_rows = jnp.repeat(block_bias, ROWS_DEV, axis=0)
    noise = 0.5 * jax.random.normal(noise_key, (ROWS, D), jnp.float32)
    return (recon + noise + bias_rows).astype(jnp.bfloat16)


def place_ends(result, own_key, least, largest):
    shape = result.shape
    index_at = [jax.random.randint(jax.random.fold_in(own_key, axis), (), 0, shape[axis]) for axis in range(len(shape))]
    result = result.at[tuple(index_at)].set(least)
    longest = shape.index(max(shape))
    index_at[longest] = (index_at[longest] + 1) % shape[longest]
    return result.at[tuple(index_at)].set(largest)


def block_levels(rng, dims, split, smallest, high):
    level = 1.0
    for position, blocks in split:
        heights = jax.random.uniform(jax.random.fold_in(jax.random.fold_in(rng, 6), position), (blocks,), jnp.float32, smallest / len(split), high / len(split))
        level = level * jnp.repeat(jnp.exp(heights), dims[position] // blocks).reshape((-1,) + (1,) * (len(dims) - 1 - position))
    return level


def deal_out(rng, own, number, rows, amount, top, most, lean):
    sequence = jax.random.permutation(rng, amount)
    packed, common = portions_of(amount, rows * top, most, lean, True), portions_of(amount, rows * top, most, lean, False)
    places = jnp.arange(amount)

    def named(sizes, rotation):
        used = int((sizes > 0).sum())
        fixed = max(1, used // 4)
        shifted = fixed + (places - fixed + rotation * (used - fixed)) % max(1, amount - fixed)
        return jnp.zeros((amount,), jnp.int32).at[sequence[jnp.where(places < fixed, places, shifted)]].set(jnp.asarray(sizes, jnp.int32))

    sizes = jnp.where(number % 4 == 0, named(packed, number // 4), named(common, number - number // 4 - 1))
    mixed = jax.random.permutation(jax.random.fold_in(own, 3), amount)
    source_of, taker = mixed[0:amount // 2 * 2:2], mixed[1:amount // 2 * 2:2]
    slack = jnp.minimum(sizes[source_of] - 1, most - sizes[taker]) // 2
    slack = jnp.where((source_of == sequence[0]) | (taker == sequence[0]) | (sizes[taker] == 0), 0, jnp.maximum(slack, 0))
    shifted = jax.random.randint(jax.random.fold_in(own, 4), (amount // 2,), 0, 1 << 20) % (slack + 1)
    sizes = sizes.at[source_of].add(-shifted).at[taker].add(shifted)
    labels = jnp.searchsorted(jnp.cumsum(sizes), jnp.arange(rows * top), side="right").astype(jnp.int32)
    listing = labels.reshape(top, rows).T
    listing = listing[jax.random.permutation(jax.random.fold_in(own, 1), rows)]
    rotation = jax.random.randint(jax.random.fold_in(own, 2), (rows, 1), 0, top)
    return jnp.take_along_axis(listing, (jnp.arange(top)[None, :] + rotation) % top, axis=1)


def portions_of(count, total, limit, skew, full):
    portions = [(1 << 20) // math.isqrt(rank ** skew) + 1 for rank in range(1, count + 1)]
    largest = limit if full else min(limit, max(-(-total // count), total * portions[0] // sum(portions)))
    least = 1 if total - largest >= count - 1 else 0
    given, spare = [largest] + [least] * (count - 1), total - largest - least * (count - 1)
    while spare > 0:
        candidates = [i for i in range(1, count) if given[i] < largest] or [i for i in range(1, count) if given[i] < limit]
        whole, remaining = sum([portions[i] for i in candidates]), spare
        for i in candidates:
            addition = min(limit - given[i], max(1, remaining * portions[i] // whole), spare)
            given[i] = given[i] + addition
            spare = spare - addition
    return np.array(given)


def centred(own_key, extent, width, most, shards=(), kind=jnp.bfloat16):
    array = width * jax.random.normal(own_key, extent, jnp.float32)
    if shards:
        array = array * block_levels(own_key, extent, shards, -0.22, 0.18)
    return jnp.clip(array, -most, most).astype(kind)


def setup_inputs(seed: int = 0) -> dict:
    key_list = jax.random.split(jax.random.key(seed), 8)
    memory_rows = draw_memory_rows(jax.random.fold_in(key_list[7], 71), 0)
    list_owner_keys = jax.random.split(jax.random.fold_in(key_list[1], 1), ROWS // ROWS_DEV)
    list_owner_turns = jax.random.permutation(jax.random.fold_in(key_list[1], 3), ROWS // ROWS_DEV)
    list_owner = jax.vmap(lambda own, number: deal_out(jax.random.fold_in(key_list[1], 2), own, number, ROWS_DEV, N_LIST, 1, CAP, 2))(list_owner_keys, list_owner_turns).reshape((ROWS, 1))
    list_slot = place_ends(jax.random.randint(key_list[2], (ROWS,), 0, LIST_DEV), jax.random.fold_in(key_list[2], 1), 0, LIST_DEV - 1).astype(jnp.int32)
    pq_codes = draw_pq_codes(jax.random.fold_in(key_list[7], 71), 0)
    valid_rows = place_ends(jax.random.randint(key_list[4], (DEVICES,), ROWS_DEV // 2, ROWS_DEV + 1), jax.random.fold_in(key_list[4], 1), ROWS_DEV // 2, ROWS_DEV).astype(jnp.int32)
    centroids = centred(key_list[5], (LISTS, D), 0.5, 3.0, ((0, 8),))
    codebook = draw_codebook(jax.random.fold_in(key_list[7], 71), 0)
    return {"memory_rows": memory_rows, "list_owner": list_owner, "list_slot": list_slot, "pq_codes": pq_codes, "valid_rows": valid_rows, "centroids": centroids, "codebook": codebook}


prior_weight = 4.0


def block_terms(block_rows, block_owner, block_slot, block_codes, count, centroids, codebook):
    is_live = jnp.arange(ROWS_DEV).astype(jnp.int32) < count
    list_index = (block_owner[:, 0] * LIST_DEV + block_slot).astype(jnp.int32)
    centre = centroids[list_index].astype(jnp.float32)
    residual = jnp.where(is_live[:, None], block_rows.astype(jnp.float32) - centre, 0.0)
    subspace = jnp.arange(M).astype(jnp.int32)
    recon = codebook[subspace[None, :], block_codes].reshape(ROWS_DEV, D)
    row_error = jnp.where(is_live, jnp.mean((residual - recon) ** 2, axis=1), 0.0)
    rounded = lax.optimization_barrier(residual.astype(jnp.bfloat16)).astype(jnp.float32)
    flat_ids = (subspace[None, :] * K + block_codes).astype(jnp.int32).reshape(-1)
    sums = jax.ops.segment_sum(rounded.reshape(ROWS_DEV * M, DS), flat_ids, M * K).reshape(M, K, DS)
    live_float = jnp.repeat(is_live.astype(jnp.float32), M)
    counts = jax.ops.segment_sum(live_float, flat_ids, M * K).reshape(M, K)
    return row_error, sums, counts


def reference(memory_rows, list_owner, list_slot, pq_codes, valid_rows, centroids, codebook):
    blocks = ROWS // ROWS_DEV
    inputs = (memory_rows.reshape(blocks, ROWS_DEV, D), list_owner.reshape(blocks, ROWS_DEV, 1),
              list_slot.reshape(blocks, ROWS_DEV), pq_codes.reshape(blocks, ROWS_DEV, M), valid_rows)

    def step(carry, item):
        row_error, sums, counts = block_terms(item[0], item[1], item[2], item[3], item[4], centroids, codebook)
        return (carry[0] + sums, carry[1] + counts), row_error

    start = (jnp.zeros((M, K, DS), jnp.float32), jnp.zeros((M, K), jnp.float32))
    totals, errors = lax.scan(step, start, inputs)
    new_codebook = (totals[0] + prior_weight * codebook) / (totals[1][:, :, None] + prior_weight)
    return new_codebook, errors.reshape(ROWS)
```

```python
import functools

import jax
import jax.numpy as jnp
from jax import lax
from jax.experimental import pallas as pl
from jax.experimental.pallas import tpu as pltpu
from jax.sharding import PartitionSpec as P

prior_weight = 4.0
F32, BF16, I32 = jnp.float32, jnp.bfloat16, jnp.int32
VMEM = pl.BlockSpec(memory_space=pltpu.VMEM)
SMEM = pl.BlockSpec(memory_space=pltpu.SMEM)
NT = (((1,), (1,)), ((), ()))
extra = 16


def mask_bf16(mask):
    return jnp.where(mask, 1.0, 0.0).astype(BF16)


def dot(a, b):
    return jnp.dot(a, b, preferred_element_type=F32)


def dot_nt(a, b):
    return lax.dot_general(a, b, NT, preferred_element_type=F32)


def pack_kernel(owners, replicas, capacity, place, valid, rows, owner, slot, codes, *outs):
    pieces = outs[:owners]
    blocks = outs[owners : owners + replicas]
    requests, position_out = outs[owners + replicas :]
    row_count, width = rows.shape
    me, rep = place[0], place[1]
    lane = lax.broadcasted_iota(I32, (1, row_count), 1)
    live = lane < valid[0]
    target = jnp.where(live, owner[...], -1)
    hit = jnp.where(lax.broadcasted_iota(I32, (owners, row_count), 0) == target, 1.0, 0.0)
    earlier = mask_bf16(
        lax.broadcasted_iota(I32, (row_count, row_count), 0)
        < lax.broadcasted_iota(I32, (row_count, row_count), 1)
    )
    before = dot(hit.astype(BF16), earlier)
    rank = jnp.sum(hit * before, axis=0, keepdims=True).astype(I32)
    position = jnp.where(live, target * capacity + rank, -1)
    position_out[...] = position

    code_rows = codes[...].astype(F32)
    high = (slot[...] // 256).astype(F32)
    low = (slot[...] % 256).astype(F32)
    which = lax.broadcasted_iota(I32, (extra, row_count), 0)
    tail = jnp.where(which == 0, high, jnp.where(which == 1, low, jnp.where(which == 2, 1.0, 0.0)))
    info = jnp.concatenate([code_rows, tail], axis=0).astype(BF16)
    within = lax.broadcasted_iota(I32, (capacity, row_count), 0)
    for step in range(owners):
        dest = jnp.bitwise_xor(me, step)
        place_at = mask_bf16(within == position - dest * capacity)
        pieces[step][...] = dot(place_at, rows[...]).astype(BF16)
        asked = dot_nt(info, place_at).astype(BF16)
        for r in range(replicas):
            requests[dest * replicas + r] = asked

    share = width // replicas
    live_codes = jnp.where(live, code_rows, 256.0).astype(BF16)
    subs = codes.shape[0]
    for step in range(replicas):
        group = jnp.bitwise_xor(rep, step)
        start = pl.multiple_of(group * share, share)
        blocks[step][0:row_count, :] = rows[:, pl.ds(start, share)]
        for part in range(row_count // share):
            blocks[step][row_count + part * subs : row_count + (part + 1) * subs, :] = live_codes[
                :, part * share : (part + 1) * share
            ]


def sums_kernel(owners, replicas, chunk, subs, place, centres, requests, *refs):
    blocks = refs[:replicas]
    keep, send, total, turned = refs[replicas:]
    lists, share = centres.shape
    sources, request_rows, capacity = requests.shape
    group_subs, _, code_count = total.shape
    width_sub = share // group_subs
    rep = place[1]
    turned[...] = centres[...].T
    span = chunk * capacity

    def pick(rows_in):
        at = lax.broadcasted_iota(I32, (8, rows_in), 0)
        col = lax.broadcasted_iota(I32, (8, rows_in), 1)
        return mask_bf16((col == rep * group_subs + at) & (at < group_subs))

    pick_asked = pick(request_rows)
    pick_local = pick(subs)
    code_iota = lax.broadcasted_iota(I32, (code_count, span), 0)
    low_iota = lax.broadcasted_iota(I32, (256, span), 0)
    total[...] = jnp.zeros_like(total)

    @pl.loop(0, sources // chunk)
    def _(index):
        asked = jnp.concatenate([requests[index * chunk + j] for j in range(chunk)], axis=1)
        codes = dot(pick_asked, asked).astype(I32)
        asked32 = asked[subs : subs + extra].astype(F32)
        high = asked32[0:1].astype(I32)
        low = asked32[1:2].astype(I32)
        live = asked32[2:3] > 0.5
        low_hit = mask_bf16(low_iota == jnp.where(live, low, -1))
        slot_hit = jnp.concatenate(
            [low_hit * mask_bf16(high == h) for h in range(lists // 256)], axis=0
        )
        gathered = dot(turned[...], slot_hit).astype(BF16)
        for m in range(group_subs):
            code_hit = mask_bf16(code_iota == codes[m : m + 1])
            total[m, 0:width_sub] -= dot_nt(
                gathered[m * width_sub : (m + 1) * width_sub], code_hit
            )

    row_count = (blocks[0].shape[0] * share) // (share + subs)
    local_iota = lax.broadcasted_iota(I32, (code_count, row_count), 0)
    ones = jnp.ones((16, row_count), BF16)
    half = group_subs // 2
    mine = jnp.bitwise_and(place[0], 1)
    hits = []
    for block in blocks:
        columns = block[0:row_count, :].T
        local = jnp.concatenate(
            [
                block[row_count + p * subs : row_count + (p + 1) * subs, :]
                for p in range(row_count // share)
            ],
            axis=1,
        )
        codes = dot(pick_local, local).astype(I32)
        hits.append((columns, codes))
    for m in range(group_subs):
        sums = total[m, 0:width_sub]
        counts = jnp.zeros((16, code_count), F32)
        for columns, codes in hits:
            code_hit = mask_bf16(local_iota == codes[m : m + 1])
            sums += dot_nt(columns[m * width_sub : (m + 1) * width_sub], code_hit)
            counts += dot_nt(ones, code_hit)

        def store(out):
            out[m % half, 0:width_sub] = sums
            out[m % half, width_sub : width_sub + 8] = counts[0:8]

        pl.when(mine == m // half)(functools.partial(store, keep))
        pl.when(mine != m // half)(functools.partial(store, send))


def target_kernel(subs, place, requests, centres, book, out):
    lists = centres.shape[0]
    width_sub, code_count = book.shape[1:]
    chunk, _, capacity = requests.shape
    span = chunk * capacity
    asked = jnp.concatenate([requests[j] for j in range(chunk)], axis=1).astype(F32)
    turned = asked.T.astype(I32)
    slots = turned[:, subs : subs + 1] * 256 + turned[:, subs + 1 : subs + 2]
    slot_hit = mask_bf16(lax.broadcasted_iota(I32, (span, lists), 1) == slots)
    centre = dot(slot_hit, centres[...])
    code_iota = lax.broadcasted_iota(I32, (span, code_count), 1)
    empty = jnp.zeros((width_sub, code_count), BF16)
    for pair in range(subs // 2):
        hits, highs, lows = [], [], []
        for m in (2 * pair, 2 * pair + 1):
            hits.append(mask_bf16(code_iota == turned[:, m : m + 1]))
            high = book[m].astype(BF16)
            highs.append(high)
            lows.append((book[m] - high.astype(F32)).astype(BF16))
        table = jnp.concatenate(
            [
                jnp.concatenate([highs[0], empty], axis=1),
                jnp.concatenate([empty, highs[1]], axis=1),
                jnp.concatenate([lows[0], empty], axis=1),
                jnp.concatenate([empty, lows[1]], axis=1),
            ],
            axis=0,
        )
        recon = dot_nt(jnp.concatenate(hits, axis=1), table)
        lanes = 2 * width_sub
        out[:, pair * lanes : (pair + 1) * lanes] = (
            centre[:, pair * lanes : (pair + 1) * lanes] + recon[:, :lanes] + recon[:, lanes:]
        )


def error_kernel(owners, place, targets, *refs):
    pieces, out = refs[:owners], refs[owners]
    capacity, width = pieces[0].shape
    for step in range(owners):
        source = jnp.bitwise_xor(place[0], step)
        start = pl.multiple_of(source * capacity, capacity)
        partial = jnp.zeros((capacity, 128), F32)
        for column in range(0, width, 128):
            gap = (
                pieces[step][:, column : column + 128].astype(F32)
                - targets[pl.ds(start, capacity), column : column + 128]
            )
            partial += gap * gap
        out[source] = jnp.sum(partial.T, axis=0, keepdims=True) * (1.0 / width)


def unpack_kernel(returned, position, out):
    owners, _, capacity = returned.shape
    row_count = position.shape[1]
    table = jnp.concatenate([returned[o] for o in range(owners)], axis=0).T
    within = lax.broadcasted_iota(I32, (capacity, row_count), 0)
    found = jnp.zeros((capacity, row_count), F32)
    for o in range(owners):
        found += jnp.where(within == position[...] - o * capacity, table[:, o : o + 1], 0.0)
    out[...] = jnp.sum(found, axis=0, keepdims=True)


def refresh_kernel(place, own, other, book, out):
    half, _, code_count = own.shape
    width_sub = book.shape[1]
    mine = jnp.bitwise_and(place[0], 1)
    for index, part in ((mine, own), (1 - mine, other)):
        for i in range(half):
            m = index * half + i
            sums, counts = part[i, 0:width_sub], part[i, width_sub : width_sub + 1]
            out[m] = (sums + prior_weight * book[m]) / (counts + prior_weight)


def swap(array, axis, step):
    count = lax.axis_size(axis)
    return lax.ppermute(array, axis, [(i, i ^ step) for i in range(count)])


def struct(*shape, dtype=F32):
    return jax.ShapeDtypeStruct(shape, dtype)


def params(mib):
    return pltpu.CompilerParams(vmem_limit_bytes=mib << 20)


def cost(flops, size):
    return pl.CostEstimate(flops=int(flops), bytes_accessed=int(size), transcendentals=0)


def body(memory_rows, list_owner, list_slot, pq_codes, valid_rows, centroids, codebook):
    row_count, width = memory_rows.shape
    lists = centroids.shape[0]
    subs, code_count, width_sub = codebook.shape
    owners, replicas = lax.axis_size("list"), lax.axis_size("rep")
    capacity = max(128, 4 * row_count // owners)
    share = width // replicas
    group_subs = subs // replicas
    request_rows = subs + extra
    devices = owners * replicas
    place = jnp.stack([lax.axis_index("list"), lax.axis_index("rep")]).astype(I32)
    book = jnp.transpose(codebook, (0, 2, 1))

    packed = pl.pallas_call(
        functools.partial(pack_kernel, owners, replicas, capacity),
        in_specs=[SMEM, SMEM] + [VMEM] * 4,
        out_specs=[VMEM] * (owners + replicas + 2),
        out_shape=[struct(capacity, width, dtype=BF16)] * owners
        + [struct(row_count + subs * row_count // share, share, dtype=BF16)] * replicas
        + [
            struct(devices, request_rows, capacity, dtype=BF16),
            struct(1, row_count, dtype=I32),
        ],
        compiler_params=params(40),
        cost_estimate=cost(2 * owners * capacity * row_count * width, 4 << 20),
        name="pack",
    )(
        place,
        valid_rows,
        memory_rows,
        list_owner.reshape(1, row_count),
        list_slot.reshape(1, row_count),
        pq_codes.T,
    )
    pieces = packed[:owners]
    blocks = packed[owners : owners + replicas]
    requests, position = packed[owners + replicas :]

    requests = lax.all_to_all(requests, ("list", "rep"), 0, 0, tiled=True)
    got_blocks = [blocks[0]] + [swap(blocks[s], "rep", s) for s in range(1, replicas)]
    got_pieces = [pieces[0]] + [swap(pieces[s], "list", s) for s in range(1, owners)]

    chunk = 8
    half_shape = struct(group_subs // 2, width_sub + 8, code_count)
    keep, send = pl.pallas_call(
        functools.partial(sums_kernel, owners, replicas, chunk, subs),
        grid_spec=pltpu.PrefetchScalarGridSpec(
            num_scalar_prefetch=1,
            grid=(1,),
            in_specs=[
                pl.BlockSpec((lists, share), lambda i, at: (0, at[1])),
                pl.BlockSpec((devices, request_rows, capacity), lambda i, at: (0, 0, 0)),
            ]
            + [pl.BlockSpec(b.shape, lambda i, at: (0, 0)) for b in got_blocks],
            out_specs=[pl.BlockSpec(half_shape.shape, lambda i, at: (0, 0, 0))] * 2,
            scratch_shapes=[
                pltpu.VMEM((group_subs, width_sub, code_count), F32),
                pltpu.VMEM((share, lists), BF16),
            ],
        ),
        out_shape=[half_shape] * 2,
        compiler_params=params(48),
        cost_estimate=cost(2 * devices * capacity * lists * share, 2 << 20),
        name="sums",
    )(place, centroids, requests, *got_blocks)

    own = keep + swap(send, "list", 1)
    others = [swap(own, "list", s) for s in range(2, owners, 2)]
    own = functools.reduce(jnp.add, others, own)
    other = swap(own, "list", 1)
    new_codebook = pl.pallas_call(
        refresh_kernel,
        grid_spec=pltpu.PrefetchScalarGridSpec(
            num_scalar_prefetch=1,
            grid=(1,),
            in_specs=[
                pl.BlockSpec(half_shape.shape, lambda i, at: (0, 0, 0)),
                pl.BlockSpec(half_shape.shape, lambda i, at: (0, 0, 0)),
                pl.BlockSpec((group_subs, width_sub, code_count), lambda i, at: (at[1], 0, 0)),
            ],
            out_specs=pl.BlockSpec((group_subs, width_sub, code_count), lambda i, at: (0, 0, 0)),
        ),
        out_shape=struct(group_subs, width_sub, code_count),
        cost_estimate=cost(1 << 20, 1 << 20),
        name="refresh",
    )(place, own, other, book)

    group = 4
    targets = pl.pallas_call(
        functools.partial(target_kernel, subs),
        grid_spec=pltpu.PrefetchScalarGridSpec(
            num_scalar_prefetch=1,
            grid=(owners // group,),
            in_specs=[
                pl.BlockSpec(
                    (group, None, request_rows, capacity), lambda i, at: (i, at[1], 0, 0)
                ),
                pl.BlockSpec((lists, width), lambda i, at: (0, 0)),
                pl.BlockSpec((subs, width_sub, code_count), lambda i, at: (0, 0, 0)),
            ],
            out_specs=pl.BlockSpec((group * capacity, width), lambda i, at: (i, 0)),
        ),
        out_shape=struct(owners * capacity, width),
        compiler_params=params(48),
        cost_estimate=cost(2 * owners * capacity * lists * width, 9 << 20),
        name="targets",
    )(place, requests.reshape(owners, replicas, request_rows, capacity), centroids, book)

    errors = pl.pallas_call(
        functools.partial(error_kernel, owners),
        in_specs=[SMEM] + [VMEM] * (owners + 1),
        out_specs=VMEM,
        out_shape=struct(owners, 1, capacity),
        compiler_params=params(48),
        cost_estimate=cost(4 * owners * capacity * width, 6 << 20),
        name="errors",
    )(place, targets, *got_pieces)
    returned = lax.all_to_all(errors, "list", 0, 0, tiled=True)
    row_error = pl.pallas_call(
        unpack_kernel,
        in_specs=[VMEM] * 2,
        out_specs=VMEM,
        out_shape=struct(1, row_count),
        name="unpack",
    )(returned, position)
    return (jnp.transpose(new_codebook, (0, 2, 1)), row_error.reshape(row_count))


def solution(mesh):
    in_specs = (
        P(("list", "rep"), None),
        P(("list", "rep"), None),
        P(("list", "rep")),
        P(("list", "rep"), None),
        P(("list", "rep")),
        P("list", None),
        P(),
    )
    out_specs = (P("rep", None, None), P(("list", "rep")))
    return jax.shard_map(body, mesh=mesh, in_specs=in_specs, out_specs=out_specs, check_vma=False)
```

```python
import functools

import jax
import jax.numpy as jnp
from jax import lax
from jax.experimental import pallas as pl
from jax.experimental.pallas import tpu as pltpu
from jax.sharding import PartitionSpec as P

prior_weight = 4.0
F32, BF16, I32 = jnp.float32, jnp.bfloat16, jnp.int32
VMEM = pl.BlockSpec(memory_space=pltpu.VMEM)
SMEM = pl.BlockSpec(memory_space=pltpu.SMEM)
NT = (((1,), (1,)), ((), ()))
request_rows = 16


def mask_bf16(mask):
    return jnp.where(mask, 1.0, 0.0).astype(BF16)


def dot(a, b):
    return jnp.dot(a, b, preferred_element_type=F32)


def dot_nt(a, b):
    return lax.dot_general(a, b, NT, preferred_element_type=F32)


def pack_kernel(owners, replicas, capacity, place, valid, rows, owner, slot, codes, *outs):
    blocks = outs[:replicas]
    requests, position_out = outs[replicas:]
    row_count, width = rows.shape
    rep = place[1]
    lane = lax.broadcasted_iota(I32, (1, row_count), 1)
    live = lane < valid[0]
    target = jnp.where(live, owner[...], -1)
    hit = jnp.where(lax.broadcasted_iota(I32, (owners, row_count), 0) == target, 1.0, 0.0)
    earlier = mask_bf16(
        lax.broadcasted_iota(I32, (row_count, row_count), 0)
        < lax.broadcasted_iota(I32, (row_count, row_count), 1)
    )
    before = dot(hit.astype(BF16), earlier)
    rank = jnp.sum(hit * before, axis=0, keepdims=True).astype(I32)
    position = jnp.where(live, target * capacity + rank, -1)
    position_out[...] = position

    code_rows = codes[...].astype(F32)
    subs = code_rows.shape[0]
    group_subs = subs // replicas
    high = (slot[...] // 256).astype(F32)
    low = (slot[...] % 256).astype(F32)
    which = lax.broadcasted_iota(I32, (request_rows - group_subs, row_count), 0)
    tail = jnp.where(which == 0, high, jnp.where(which == 1, low, jnp.where(which == 2, 1.0, 0.0)))
    info = jnp.concatenate(
        [
            part
            for g in range(replicas)
            for part in (code_rows[g * group_subs : (g + 1) * group_subs], tail)
        ],
        axis=0,
    ).astype(BF16)
    within = lax.broadcasted_iota(I32, (capacity, row_count), 0)
    for dest in range(owners):
        place_at = mask_bf16(within == position - dest * capacity)
        asked = dot_nt(info, place_at).astype(BF16)
        for g in range(replicas):
            requests[dest * replicas + g] = asked[g * request_rows : (g + 1) * request_rows]

    share = width // replicas
    live_codes = jnp.where(live, code_rows, 256.0).astype(BF16)
    for step in range(replicas):
        group = jnp.bitwise_xor(rep, step)
        start = pl.multiple_of(group * share, share)
        blocks[step][0:row_count, :] = rows[:, pl.ds(start, share)]
        for part in range(row_count // share):
            blocks[step][row_count + part * subs : row_count + (part + 1) * subs, :] = live_codes[
                :, part * share : (part + 1) * share
            ]


def pick(group, group_subs, rows_in):
    at = lax.broadcasted_iota(I32, (8, rows_in), 0)
    col = lax.broadcasted_iota(I32, (8, rows_in), 1)
    return mask_bf16((col == group * group_subs + at) & (at < group_subs))


def centre_sums_kernel(chunk, place, centres, requests, total, turned):
    lists, share = centres.shape
    sources, _, capacity = requests.shape
    group_subs, width_sub, code_count = total.shape
    turned[...] = centres[...].T
    span = chunk * capacity
    code_iota = lax.broadcasted_iota(I32, (code_count, span), 0)
    low_iota = lax.broadcasted_iota(I32, (256, span), 0)
    total[...] = jnp.zeros_like(total)

    @pl.loop(0, sources // chunk)
    def _(index):
        asked = jnp.concatenate([requests[index * chunk + j] for j in range(chunk)], axis=1)
        asked = asked.astype(F32).astype(I32)
        codes = asked[0:group_subs]
        high, low, live = (asked[group_subs + i : group_subs + i + 1] for i in range(3))
        low_hit = mask_bf16(low_iota == jnp.where(live > 0, low, -1))
        slot_hit = jnp.concatenate(
            [low_hit * mask_bf16(high == h) for h in range(lists // 256)], axis=0
        )
        gathered = dot(turned[...], slot_hit).astype(BF16)
        for m in range(group_subs):
            code_hit = mask_bf16(code_iota == codes[m : m + 1])
            total[m] += dot_nt(gathered[m * width_sub : (m + 1) * width_sub], code_hit)


def row_sums_kernel(replicas, subs, place, centre_sums, book, *refs):
    blocks = refs[:replicas]
    keep, send = refs[replicas:]
    group_subs, width_sub, code_count = centre_sums.shape
    share = width_sub * group_subs
    pick_local = pick(place[1], group_subs, subs)
    row_count = (blocks[0].shape[0] * share) // (share + subs)
    local_iota = lax.broadcasted_iota(I32, (code_count, row_count), 0)
    ones = jnp.ones((16, row_count), BF16)
    prior = jnp.where(place[0] == 0, prior_weight, 0.0)
    half = group_subs // 2
    mine = jnp.bitwise_and(place[0], 1)
    hits = []
    for block in blocks:
        columns = block[0:row_count, :].T
        local = jnp.concatenate(
            [
                block[row_count + p * subs : row_count + (p + 1) * subs, :]
                for p in range(row_count // share)
            ],
            axis=1,
        )
        codes = dot(pick_local, local).astype(I32)
        hits.append((columns, codes))
    for m in range(group_subs):
        sums = prior * book[m] - centre_sums[m]
        counts = jnp.full((16, code_count), prior, F32)
        for columns, codes in hits:
            code_hit = mask_bf16(local_iota == codes[m : m + 1])
            sums += dot_nt(columns[m * width_sub : (m + 1) * width_sub], code_hit)
            counts += dot_nt(ones, code_hit)

        def store(out):
            out[m % half, 0:width_sub] = sums
            out[m % half, width_sub : width_sub + 8] = counts[0:8]

        pl.when(mine == m // half)(functools.partial(store, keep))
        pl.when(mine != m // half)(functools.partial(store, send))


def gather_kernel(group_subs, place, requests, centres, out):
    lists = centres.shape[0]
    chunk, _, capacity = requests.shape
    span = chunk * capacity
    asked = jnp.concatenate([requests[j] for j in range(chunk)], axis=1).astype(F32)
    turned = asked.T.astype(I32)
    slots = turned[:, group_subs : group_subs + 1] * 256 + turned[:, group_subs + 1 : group_subs + 2]
    slot_hit = mask_bf16(lax.broadcasted_iota(I32, (span, lists), 1) == slots)
    out[...] = dot(slot_hit, centres[...]).astype(BF16)


def offset_kernel(rows, codes, book, out):
    subs, width_sub, code_count = book.shape
    row_count = rows.shape[0]
    turned = codes[...].astype(F32).T.astype(I32)
    code_iota = lax.broadcasted_iota(I32, (row_count, code_count), 1)
    empty = jnp.zeros((width_sub, code_count), BF16)
    for pair in range(subs // 2):
        hits, highs, lows = [], [], []
        for m in (2 * pair, 2 * pair + 1):
            hits.append(mask_bf16(code_iota == turned[:, m : m + 1]))
            high = book[m].astype(BF16)
            highs.append(high)
            lows.append((book[m] - high.astype(F32)).astype(BF16))
        table = jnp.concatenate(
            [
                jnp.concatenate([highs[0], empty], axis=1),
                jnp.concatenate([empty, highs[1]], axis=1),
                jnp.concatenate([lows[0], empty], axis=1),
                jnp.concatenate([empty, lows[1]], axis=1),
            ],
            axis=0,
        )
        recon = dot_nt(jnp.concatenate(hits, axis=1), table)
        lanes = 2 * width_sub
        span = slice(pair * lanes, (pair + 1) * lanes)
        out[:, span] = rows[:, span].astype(F32) - (recon[:, :lanes] + recon[:, lanes:])


def error_kernel(valid, position, offsets, centres, out):
    slots, width = centres.shape
    row_count = offsets.shape[0]
    column_at = jnp.broadcast_to(position[...].astype(F32), (8, row_count)).T.astype(I32)[:, 0:1]
    hit = mask_bf16(lax.broadcasted_iota(I32, (row_count, slots), 1) == column_at)
    partial = jnp.zeros((row_count, 128), F32)
    for start in range(0, width, 256):
        gap = offsets[:, start : start + 256] - dot(hit, centres[:, start : start + 256])
        square = gap * gap
        partial += square[:, :128] + square[:, 128:]
    error = jnp.sum(partial.T, axis=0, keepdims=True) * (1.0 / width)
    lane = lax.broadcasted_iota(I32, (1, row_count), 1)
    out[...] = jnp.where(lane < valid[0], error, 0.0)


def swap(array, axis, step):
    count = lax.axis_size(axis)
    return lax.ppermute(array, axis, [(i, i ^ step) for i in range(count)])


def struct(*shape, dtype=F32):
    return jax.ShapeDtypeStruct(shape, dtype)


def params(mib):
    return pltpu.CompilerParams(vmem_limit_bytes=mib << 20)


def cost(flops, size):
    return pl.CostEstimate(flops=int(flops), bytes_accessed=int(size), transcendentals=0)


def body(memory_rows, list_owner, list_slot, pq_codes, valid_rows, centroids, codebook):
    row_count, width = memory_rows.shape
    lists = centroids.shape[0]
    subs, code_count, width_sub = codebook.shape
    owners, replicas = lax.axis_size("list"), lax.axis_size("rep")
    capacity = max(128, 4 * row_count // owners)
    share = width // replicas
    group_subs = subs // replicas
    devices = owners * replicas
    place = jnp.stack([lax.axis_index("list"), lax.axis_index("rep")]).astype(I32)
    book = jnp.transpose(codebook, (0, 2, 1))

    codes = pq_codes.T

    packed = pl.pallas_call(
        functools.partial(pack_kernel, owners, replicas, capacity),
        in_specs=[SMEM, SMEM] + [VMEM] * 4,
        out_specs=[VMEM] * (replicas + 2),
        out_shape=[struct(row_count + subs * row_count // share, share, dtype=BF16)] * replicas
        + [
            struct(devices, request_rows, capacity, dtype=BF16),
            struct(1, row_count, dtype=I32),
        ],
        compiler_params=params(60),
        cost_estimate=cost(1 << 20, 1 << 20),
        name="pack",
    )(
        place,
        valid_rows,
        memory_rows,
        list_owner.reshape(1, row_count),
        list_slot.reshape(1, row_count),
        codes,
    )
    blocks = packed[:replicas]
    requests, position = packed[replicas:]

    requests = lax.all_to_all(requests, ("list", "rep"), 0, 0, tiled=True)
    got_blocks = [blocks[0]] + [swap(blocks[s], "rep", s) for s in range(1, replicas)]

    group = 4
    gathered = pl.pallas_call(
        functools.partial(gather_kernel, group_subs),
        grid_spec=pltpu.PrefetchScalarGridSpec(
            num_scalar_prefetch=1,
            grid=(owners // group,),
            in_specs=[
                pl.BlockSpec(
                    (group, None, request_rows, capacity), lambda i, at: (i, at[1], 0, 0)
                ),
                pl.BlockSpec((lists, width), lambda i, at: (0, 0)),
            ],
            out_specs=pl.BlockSpec((group * capacity, width), lambda i, at: (i, 0)),
        ),
        out_shape=struct(owners * capacity, width, dtype=BF16),
        compiler_params=params(48),
        cost_estimate=cost(2 * owners * capacity * lists * width, 6 << 20),
        name="gather",
    )(place, requests.reshape(owners, replicas, request_rows, capacity), centroids)
    centres = lax.all_to_all(
        gathered.reshape(owners, capacity, width), "list", 0, 0, tiled=True
    ).reshape(owners * capacity, width)

    chunk = 8
    half_shape = struct(group_subs // 2, width_sub + 8, code_count)
    centre_sums = pl.pallas_call(
        functools.partial(centre_sums_kernel, chunk),
        grid_spec=pltpu.PrefetchScalarGridSpec(
            num_scalar_prefetch=1,
            grid=(1,),
            in_specs=[
                pl.BlockSpec((lists, share), lambda i, at: (0, at[1])),
                pl.BlockSpec((devices, request_rows, capacity), lambda i, at: (0, 0, 0)),
            ],
            out_specs=pl.BlockSpec((group_subs, width_sub, code_count), lambda i, at: (0, 0, 0)),
            scratch_shapes=[pltpu.VMEM((share, lists), BF16)],
        ),
        out_shape=struct(group_subs, width_sub, code_count),
        compiler_params=params(48),
        cost_estimate=cost(2 * devices * capacity * lists * share, 2 << 20),
        name="centre_sums",
    )(place, centroids, requests)
    keep, send = pl.pallas_call(
        functools.partial(row_sums_kernel, replicas, subs),
        grid_spec=pltpu.PrefetchScalarGridSpec(
            num_scalar_prefetch=1,
            grid=(1,),
            in_specs=[
                pl.BlockSpec((group_subs, width_sub, code_count), lambda i, at: (0, 0, 0)),
                pl.BlockSpec((group_subs, width_sub, code_count), lambda i, at: (at[1], 0, 0)),
            ]
            + [pl.BlockSpec(b.shape, lambda i, at: (0, 0)) for b in got_blocks],
            out_specs=[pl.BlockSpec(half_shape.shape, lambda i, at: (0, 0, 0))] * 2,
        ),
        out_shape=[half_shape] * 2,
        compiler_params=params(48),
        cost_estimate=cost(1 << 30, 2 << 20),
        name="row_sums",
    )(place, centre_sums, book, *got_blocks)

    own = keep + swap(send, "list", 1)
    others = [swap(own, "list", s) for s in range(2, owners, 2)]
    own = functools.reduce(jnp.add, others, own)
    own = own[:, :width_sub] / own[:, width_sub : width_sub + 1]
    other = swap(own, "list", 1)
    first = lax.axis_index("list") % 2 == 0
    new_codebook = jnp.concatenate(
        [jnp.where(first, own, other), jnp.where(first, other, own)], axis=0
    )

    offsets = pl.pallas_call(
        offset_kernel,
        in_specs=[VMEM] * 3,
        out_specs=VMEM,
        out_shape=struct(row_count, width),
        compiler_params=params(48),
        cost_estimate=cost(2 << 30, 2 << 20),
        name="offsets",
    )(memory_rows, codes, book)
    row_error = pl.pallas_call(
        error_kernel,
        in_specs=[SMEM] + [VMEM] * 3,
        out_specs=VMEM,
        out_shape=struct(1, row_count),
        compiler_params=params(48),
        cost_estimate=cost(2 * owners * capacity * row_count * width, 3 << 20),
        name="errors",
    )(valid_rows, position, offsets, centres)
    return (jnp.transpose(new_codebook, (0, 2, 1)), row_error.reshape(row_count))


def solution(mesh):
    in_specs = (
        P(("list", "rep"), None),
        P(("list", "rep"), None),
        P(("list", "rep")),
        P(("list", "rep"), None),
        P(("list", "rep")),
        P("list", None),
        P(),
    )
    out_specs = (P("rep", None, None), P(("list", "rep")))
    return jax.shard_map(body, mesh=mesh, in_specs=in_specs, out_specs=out_specs, check_vma=False)
```

```python
import functools

import jax
import jax.numpy as jnp
from jax import lax
from jax.experimental import pallas as pl
from jax.experimental.pallas import tpu as pltpu
from jax.sharding import PartitionSpec as P

prior_weight = 4.0
F32, BF16, I32 = jnp.float32, jnp.bfloat16, jnp.int32
VMEM = pl.BlockSpec(memory_space=pltpu.VMEM)
ANY = pl.BlockSpec(memory_space=pl.ANY)
SMEM = pl.BlockSpec(memory_space=pltpu.SMEM)
NT = (((1,), (1,)), ((), ()))
extra = 16


def mask_bf16(mask):
    return jnp.where(mask, 1.0, 0.0).astype(BF16)


def dot(a, b):
    return jnp.dot(a, b, preferred_element_type=F32)


def dot_nt(a, b):
    return lax.dot_general(a, b, NT, preferred_element_type=F32)


def pack_kernel(owners, capacity, valid, owner, slot, codes, requests, position_out):
    row_count = owner.shape[1]
    lane = lax.broadcasted_iota(I32, (1, row_count), 1)
    live = lane < valid[0]
    target = jnp.where(live, owner[...], -1)
    hit = jnp.where(lax.broadcasted_iota(I32, (owners, row_count), 0) == target, 1.0, 0.0)
    earlier = mask_bf16(
        lax.broadcasted_iota(I32, (row_count, row_count), 0)
        < lax.broadcasted_iota(I32, (row_count, row_count), 1)
    )
    before = dot(hit.astype(BF16), earlier)
    rank = jnp.sum(hit * before, axis=0, keepdims=True).astype(I32)
    position = jnp.where(live, target * capacity + rank, -1)
    position_out[...] = position

    high = (slot[...] // 256).astype(F32)
    low = (slot[...] % 256).astype(F32)
    which = lax.broadcasted_iota(I32, (extra, row_count), 0)
    tail = jnp.where(which == 0, high, jnp.where(which == 1, low, 0.0))
    info = jnp.concatenate([codes[...].astype(F32) - 256.0, tail], axis=0).astype(BF16)
    within = lax.broadcasted_iota(I32, (capacity, row_count), 0)
    for dest in range(owners):
        place_at = mask_bf16(within == position - dest * capacity)
        requests[dest] = dot_nt(info, place_at).astype(BF16)


def row_sums_kernel(valid, rows, codes, out):
    subs, padded, code_count = out.shape
    row_count, width = rows.shape
    width_sub = width // subs
    lane = lax.broadcasted_iota(I32, (1, row_count), 1)
    live_codes = jnp.where(lane < valid[0], codes[...], -1)
    columns = rows[...].T
    code_iota = lax.broadcasted_iota(I32, (code_count, row_count), 0)
    ones = jnp.ones((16, row_count), BF16)
    for m in range(subs):
        code_hit = mask_bf16(code_iota == live_codes[m : m + 1])
        out[m, 0:width_sub] = dot_nt(columns[m * width_sub : (m + 1) * width_sub], code_hit)
        out[m, width_sub:padded] = dot_nt(ones, code_hit)[0 : padded - width_sub]


def sums_kernel(replicas, requests, gathered, row_sums, keep, send):
    subs, padded, code_count = row_sums.shape
    owners, _, capacity = requests.shape
    slots, width = gathered.shape
    width_sub = width // subs
    group_subs = subs // replicas
    half = group_subs // 2
    mine = jnp.bitwise_and(lax.axis_index("list"), 1)
    rep = lax.axis_index("rep")
    asked = jnp.concatenate([requests[j] for j in range(owners)], axis=1)
    codes = asked.astype(F32).astype(I32) + 256
    code_iota = lax.broadcasted_iota(I32, (code_count, slots), 0)
    first = lax.broadcasted_iota(I32, (code_count, 2 * width_sub), 1) < width_sub
    for pair in range(subs // 2):
        span = slice(pair * 2 * width_sub, (pair + 1) * 2 * width_sub)
        found = [
            dot(mask_bf16(code_iota == codes[m : m + 1]), gathered[:, span])
            for m in (2 * pair, 2 * pair + 1)
        ]
        centre_sums = jnp.where(first, found[0], found[1]).T
        for j in range(2):
            m = 2 * pair + j
            sums = row_sums[m, 0:width_sub] - centre_sums[j * width_sub : (j + 1) * width_sub]
            counts = row_sums[m, width_sub:padded]
            group, at = m // group_subs, m % group_subs
            step = jnp.bitwise_xor(rep, group)

            def store(out, sums=sums, counts=counts, step=step, at=at):
                out[step, at % half, 0:width_sub] = sums
                out[step, at % half, width_sub:padded] = counts

            pl.when(mine == at // half)(functools.partial(store, keep))
            pl.when(mine != at // half)(functools.partial(store, send))


def gather_kernel(subs, requests, centres, pieces, near, hit, found, read, written):
    owners, _, capacity = requests.shape
    slots, lists = hit.shape
    loads = []
    for part in range(read.shape[0]):
        rows = pl.ds(part * (lists // read.shape[0]), lists // read.shape[0])
        loads.append(pltpu.make_async_copy(centres.at[rows], near.at[rows], read.at[part]))
        loads[-1].start()
    chunk = 4
    span = chunk * capacity
    for first in range(0, owners, chunk):
        asked = jnp.concatenate([requests[first + j] for j in range(chunk)], axis=1)
        turned = asked.astype(F32).T.astype(I32)
        high, low = (turned[:, subs + i : subs + i + 1] for i in range(2))
        low_hit = mask_bf16(lax.broadcasted_iota(I32, (span, 256), 1) == low)
        for h in range(lists // 256):
            hit[first * capacity : first * capacity + span, h * 256 : (h + 1) * 256] = (
                low_hit * mask_bf16(high == h)
            )
    for load in loads:
        load.wait()
    stores = []
    for index in range(owners // chunk):
        part = dot(hit[index * span : (index + 1) * span], near[...]).astype(BF16)
        found[index * chunk : (index + 1) * chunk] = part.reshape((chunk, *found.shape[1:]))
        block = pl.ds(index * chunk, chunk)
        stores.append(
            pltpu.make_async_copy(found.at[block], pieces.at[block], written.at[index])
        )
        stores[-1].start()
    for store in stores:
        store.wait()


def offset_kernel(rows, codes, book, out):
    subs, width_sub, code_count = book.shape
    row_count = rows.shape[0]
    turned = codes[...].astype(F32).T.astype(I32)
    code_iota = lax.broadcasted_iota(I32, (row_count, code_count), 1)
    empty = jnp.zeros((width_sub, code_count), BF16)
    for pair in range(subs // 2):
        hits, highs, lows = [], [], []
        for m in (2 * pair, 2 * pair + 1):
            hits.append(mask_bf16(code_iota == turned[:, m : m + 1]))
            high = book[m].astype(BF16)
            highs.append(high)
            lows.append((book[m] - high.astype(F32)).astype(BF16))
        table = jnp.concatenate(
            [
                jnp.concatenate([highs[0], empty], axis=1),
                jnp.concatenate([empty, highs[1]], axis=1),
                jnp.concatenate([lows[0], empty], axis=1),
                jnp.concatenate([empty, lows[1]], axis=1),
            ],
            axis=0,
        )
        recon = dot_nt(jnp.concatenate(hits, axis=1), table)
        lanes = 2 * width_sub
        span = slice(pair * lanes, (pair + 1) * lanes)
        out[:, span] = rows[:, span].astype(F32) - (recon[:, :lanes] + recon[:, lanes:])


def error_kernel(valid, position, offsets, centres, out):
    slots, width = centres.shape
    row_count = offsets.shape[0]
    column_at = jnp.broadcast_to(position[...].astype(F32), (8, row_count)).T.astype(I32)[:, 0:1]
    hit = mask_bf16(lax.broadcasted_iota(I32, (row_count, slots), 1) == column_at)
    partial = jnp.zeros((row_count, 128), F32)
    for start in range(0, width, 256):
        gap = offsets[:, start : start + 256] - dot(hit, centres[:, start : start + 256])
        square = gap * gap
        partial += square[:, :128] + square[:, 128:]
    error = jnp.sum(partial.T, axis=0, keepdims=True) * (1.0 / width)
    lane = lax.broadcasted_iota(I32, (1, row_count), 1)
    out[...] = jnp.where(lane < valid[0], error, 0.0)


def swap(array, axis, step):
    count = lax.axis_size(axis)
    return lax.ppermute(array, axis, [(i, i ^ step) for i in range(count)])


def struct(*shape, dtype=F32):
    return jax.ShapeDtypeStruct(shape, dtype)


def params(mib):
    return pltpu.CompilerParams(vmem_limit_bytes=mib << 20)


def cost(flops, size):
    return pl.CostEstimate(flops=int(flops), bytes_accessed=int(size), transcendentals=0)


def body(memory_rows, list_owner, list_slot, pq_codes, valid_rows, centroids, codebook):
    row_count, width = memory_rows.shape
    lists = centroids.shape[0]
    subs, code_count, width_sub = codebook.shape
    owners, replicas = lax.axis_size("list"), lax.axis_size("rep")
    capacity = max(128, 4 * row_count // owners)
    group_subs = subs // replicas
    half = group_subs // 2
    padded = width_sub + 8
    book = jnp.transpose(codebook, (0, 2, 1))
    codes = pq_codes.T

    requests, position = pl.pallas_call(
        functools.partial(pack_kernel, owners, capacity),
        in_specs=[SMEM] + [VMEM] * 3,
        out_specs=[VMEM] * 2,
        out_shape=[
            struct(owners, subs + extra, capacity, dtype=BF16),
            struct(1, row_count, dtype=I32),
        ],
        compiler_params=params(60),
        cost_estimate=cost(1000, 1000),
        name="pack",
    )(
        valid_rows,
        list_owner.reshape(1, row_count),
        list_slot.reshape(1, row_count),
        codes,
    )
    requests = lax.all_to_all(requests, "list", 0, 0, tiled=True)

    row_sums = pl.pallas_call(
        row_sums_kernel,
        in_specs=[SMEM] + [VMEM] * 2,
        out_specs=VMEM,
        out_shape=struct(subs, padded, code_count),
        compiler_params=params(40),
        cost_estimate=cost(1000, 1000),
        name="row_sums",
    )(valid_rows, memory_rows, codes)
    offsets = pl.pallas_call(
        offset_kernel,
        in_specs=[VMEM] * 3,
        out_specs=VMEM,
        out_shape=struct(row_count, width),
        compiler_params=params(48),
        cost_estimate=cost(1000, 1000),
        name="offsets",
    )(memory_rows, codes, book)
    requests, row_sums = lax.optimization_barrier((requests, row_sums))
    gathered = pl.pallas_call(
        functools.partial(gather_kernel, subs),
        in_specs=[VMEM, ANY],
        out_specs=ANY,
        out_shape=struct(owners, capacity, width, dtype=BF16),
        scratch_shapes=[
            pltpu.VMEM((lists, width), BF16),
            pltpu.VMEM((owners * capacity, lists), BF16),
            pltpu.VMEM((owners, capacity, width), BF16),
            pltpu.SemaphoreType.DMA((8,)),
            pltpu.SemaphoreType.DMA((owners // 4,)),
        ],
        compiler_params=params(60),
        cost_estimate=cost(4 << 30, 6 << 20),
        name="gather",
    )(requests, centroids)
    pieces = lax.all_to_all(gathered, "list", 0, 0, tiled=True)

    half_shape = struct(replicas, half, padded, code_count)
    keep, send = pl.pallas_call(
        functools.partial(sums_kernel, replicas),
        in_specs=[VMEM] * 3,
        out_specs=[VMEM] * 2,
        out_shape=[half_shape] * 2,
        compiler_params=params(40),
        cost_estimate=cost(1000, 1000),
        name="sums",
    )(requests, gathered.reshape(owners * capacity, width), row_sums)

    own = keep + swap(send, "list", 1)
    row = lax.broadcasted_iota(I32, own.shape, 2)
    high = jnp.floor(own * (1.0 / 256.0))
    own = jnp.where(
        row < width_sub, own, jnp.where(row == width_sub, high, own - 256.0 * high)
    )
    own = own[0] + sum(
        swap(own[s].astype(BF16), "rep", s).astype(F32) for s in range(1, replicas)
    )
    own, offsets = lax.optimization_barrier((own, offsets))
    others = [swap(own, "list", s) for s in range(2, owners, 2)]
    pieces, *others = lax.optimization_barrier((pieces, *others))
    own = functools.reduce(jnp.add, others, own)
    core = lax.axis_index("list") % 2
    start = lax.axis_index("rep") * group_subs + core * half
    prior = prior_weight * lax.dynamic_slice_in_dim(book, start, half, 0)
    counts = 256.0 * own[:, width_sub : width_sub + 1] + own[:, width_sub + 1 : width_sub + 2]
    own = (own[:, :width_sub] + prior) / (counts + prior_weight)
    other = swap(own, "list", 1)
    new_codebook = jnp.concatenate(
        [jnp.where(core == 0, own, other), jnp.where(core == 0, other, own)], axis=0
    )
    row_error = pl.pallas_call(
        error_kernel,
        in_specs=[SMEM] + [VMEM] * 3,
        out_specs=VMEM,
        out_shape=struct(1, row_count),
        compiler_params=params(48),
        cost_estimate=cost(1000, 1000),
        name="errors",
    )(valid_rows, position, offsets, pieces.reshape(owners * capacity, width))
    return (jnp.transpose(new_codebook, (0, 2, 1)), row_error.reshape(row_count))


def solution(mesh):
    in_specs = (
        P(("list", "rep"), None),
        P(("list", "rep"), None),
        P(("list", "rep")),
        P(("list", "rep"), None),
        P(("list", "rep")),
        P("list", None),
        P(),
    )
    out_specs = (P("rep", None, None), P(("list", "rep")))
    return jax.shard_map(body, mesh=mesh, in_specs=in_specs, out_specs=out_specs, check_vma=False)
```

```python
import functools

import jax
import jax.numpy as jnp
from jax import lax
from jax.experimental import pallas as pl
from jax.experimental.pallas import tpu as pltpu
from jax.sharding import PartitionSpec as P

prior_weight = 4.0
F32, BF16, I32 = jnp.float32, jnp.bfloat16, jnp.int32
VMEM = pl.BlockSpec(memory_space=pltpu.VMEM)
HBM = pl.BlockSpec(memory_space=pltpu.HBM)
SMEM = pl.BlockSpec(memory_space=pltpu.SMEM)
NT = (((1,), (1,)), ((), ()))
extra = 16


def mask_bf16(mask):
    return jnp.where(mask, 1.0, 0.0).astype(BF16)


def dot(a, b):
    return jnp.dot(a, b, preferred_element_type=F32)


def dot_nt(a, b):
    return lax.dot_general(a, b, NT, preferred_element_type=F32)


def pack_kernel(owners, capacity, valid, owner, slot, codes, requests, position_out):
    row_count = owner.shape[1]
    lane = lax.broadcasted_iota(I32, (1, row_count), 1)
    live = lane < valid[0]
    target = jnp.where(live, owner[...], -1)
    hit = jnp.where(lax.broadcasted_iota(I32, (owners, row_count), 0) == target, 1.0, 0.0)
    earlier = mask_bf16(
        lax.broadcasted_iota(I32, (row_count, row_count), 0)
        < lax.broadcasted_iota(I32, (row_count, row_count), 1)
    )
    before = dot(hit.astype(BF16), earlier)
    rank = jnp.sum(hit * before, axis=0, keepdims=True).astype(I32)
    position = jnp.where(live, target * capacity + rank, -1)
    position_out[...] = position

    high = (slot[...] // 256).astype(F32)
    low = (slot[...] % 256).astype(F32)
    which = lax.broadcasted_iota(I32, (extra, row_count), 0)
    tail = jnp.where(which == 0, high, jnp.where(which == 1, low, 0.0))
    info = jnp.concatenate([codes[...].astype(F32) - 256.0, tail], axis=0).astype(BF16)
    within = lax.broadcasted_iota(I32, (capacity, row_count), 0)
    for dest in range(owners):
        place_at = mask_bf16(within == position - dest * capacity)
        requests[dest] = dot_nt(info, place_at).astype(BF16)


def row_sums_kernel(valid, rows, codes, out):
    subs, padded, code_count = out.shape
    row_count, width = rows.shape
    width_sub = width // subs
    lane = lax.broadcasted_iota(I32, (1, row_count), 1)
    live_codes = jnp.where(lane < valid[0], codes[...], -1)
    columns = rows[...].T
    code_iota = lax.broadcasted_iota(I32, (code_count, row_count), 0)
    ones = jnp.ones((16, row_count), BF16)
    for m in range(subs):
        code_hit = mask_bf16(code_iota == live_codes[m : m + 1])
        out[m, 0:width_sub] = dot_nt(columns[m * width_sub : (m + 1) * width_sub], code_hit)
        out[m, width_sub:padded] = dot_nt(ones, code_hit)[0 : padded - width_sub]


def sums_kernel(replicas, requests, gathered, row_sums, keep, send):
    subs, padded, code_count = row_sums.shape
    owners, _, capacity = requests.shape
    slots, width = gathered.shape
    width_sub = width // subs
    group_subs = subs // replicas
    half = group_subs // 2
    mine = jnp.bitwise_and(lax.axis_index("list"), 1)
    rep = lax.axis_index("rep")
    asked = jnp.concatenate([requests[j] for j in range(owners)], axis=1)
    codes = asked.astype(F32).astype(I32) + 256
    code_iota = lax.broadcasted_iota(I32, (code_count, slots), 0)
    first = lax.broadcasted_iota(I32, (code_count, 2 * width_sub), 1) < width_sub
    for pair in range(subs // 2):
        span = slice(pair * 2 * width_sub, (pair + 1) * 2 * width_sub)
        found = [
            dot(mask_bf16(code_iota == codes[m : m + 1]), gathered[:, span])
            for m in (2 * pair, 2 * pair + 1)
        ]
        centre_sums = jnp.where(first, found[0], found[1]).T
        for j in range(2):
            m = 2 * pair + j
            sums = row_sums[m, 0:width_sub] - centre_sums[j * width_sub : (j + 1) * width_sub]
            counts = row_sums[m, width_sub:padded]
            group, at = m // group_subs, m % group_subs
            step = jnp.bitwise_xor(rep, group)

            def store(out, sums=sums, counts=counts, step=step, at=at):
                out[step, at % half, 0:width_sub] = sums
                out[step, at % half, width_sub:padded] = counts

            pl.when(mine == at // half)(functools.partial(store, keep))
            pl.when(mine != at // half)(functools.partial(store, send))


def gather_kernel(subs, requests, centres, pieces, near, found, loaded, written):
    owners, _, capacity = requests.shape
    lists = centres.shape[0]
    parts, chunks = loaded.shape[0], written.shape[0]
    chunk = owners // chunks
    span = chunk * capacity
    loads, stores = [], []
    for part in range(parts):
        rows = pl.ds(part * (lists // parts), lists // parts)
        loads.append(pltpu.make_async_copy(centres.at[rows], near.at[rows], loaded.at[part]))
        loads[-1].start()
    for index in range(chunks):
        asked = jnp.concatenate([requests[index * chunk + j] for j in range(chunk)], axis=1)
        turned = asked.astype(F32).T.astype(I32)
        high, low = (turned[:, subs + i : subs + i + 1] for i in range(2))
        low_hit = mask_bf16(lax.broadcasted_iota(I32, (span, 256), 1) == low)
        total = jnp.zeros((span, centres.shape[1]), F32)
        for part in range(parts):
            first, last = part * (lists // parts), (part + 1) * (lists // parts)
            hit = jnp.concatenate(
                [low_hit * mask_bf16(high == h) for h in range(first // 256, last // 256)], axis=1
            )
            if index == 0:
                loads[part].wait()
            total += dot(hit, near[first:last])
        block = pl.ds(index * chunk, chunk)
        found[block] = total.astype(BF16).reshape((chunk, *found.shape[1:]))
        stores.append(
            pltpu.make_async_copy(found.at[block], pieces.at[block], written.at[index])
        )
        stores[-1].start()
    for store in stores:
        store.wait()


def offset_kernel(rows, codes, book, out):
    subs, width_sub, code_count = book.shape
    row_count = rows.shape[0]
    turned = codes[...].astype(F32).T.astype(I32)
    code_iota = lax.broadcasted_iota(I32, (row_count, code_count), 1)
    empty = jnp.zeros((width_sub, code_count), BF16)
    for pair in range(subs // 2):
        hits, highs, lows = [], [], []
        for m in (2 * pair, 2 * pair + 1):
            hits.append(mask_bf16(code_iota == turned[:, m : m + 1]))
            high = book[m].astype(BF16)
            highs.append(high)
            lows.append((book[m] - high.astype(F32)).astype(BF16))
        table = jnp.concatenate(
            [
                jnp.concatenate([highs[0], empty], axis=1),
                jnp.concatenate([empty, highs[1]], axis=1),
                jnp.concatenate([lows[0], empty], axis=1),
                jnp.concatenate([empty, lows[1]], axis=1),
            ],
            axis=0,
        )
        recon = dot_nt(jnp.concatenate(hits, axis=1), table)
        lanes = 2 * width_sub
        span = slice(pair * lanes, (pair + 1) * lanes)
        out[:, span] = rows[:, span].astype(F32) - (recon[:, :lanes] + recon[:, lanes:])


def error_kernel(valid, position, offsets, centres, out):
    slots, width = centres.shape
    row_count = offsets.shape[0]
    column_at = jnp.broadcast_to(position[...].astype(F32), (8, row_count)).T.astype(I32)[:, 0:1]
    hit = mask_bf16(lax.broadcasted_iota(I32, (row_count, slots), 1) == column_at)
    partial = jnp.zeros((row_count, 128), F32)
    for start in range(0, width, 256):
        gap = offsets[:, start : start + 256] - dot(hit, centres[:, start : start + 256])
        square = gap * gap
        partial += square[:, :128] + square[:, 128:]
    error = jnp.sum(partial.T, axis=0, keepdims=True) * (1.0 / width)
    lane = lax.broadcasted_iota(I32, (1, row_count), 1)
    out[...] = jnp.where(lane < valid[0], error, 0.0)


def encode_kernel(width_sub, *refs):
    parts, out = refs[:-1], refs[-1]
    half, padded, code_count = out.shape
    which = lax.broadcasted_iota(I32, (padded - width_sub, code_count), 0)
    for m in range(half):
        total = parts[0][m]
        for part in parts[1:]:
            total += part[m].astype(F32)
        sums, counts = total[:width_sub], total[width_sub:]
        top = jnp.max(jnp.abs(sums), axis=0, keepdims=True)
        exponent = jnp.clip(jnp.ceil(jnp.log2(top)) - 1.0, -125.0, 127.0)
        scaled = jnp.clip(jnp.round(sums / jnp.exp2(exponent) * 16384.0), -32767.0, 32767.0)
        tail = jnp.where(which < 2, counts, jnp.where(which == 2, exponent, 0.0))
        out[m] = jnp.concatenate([scaled, tail], axis=0).astype(I32).astype(jnp.int16)


def swap(array, axis, step):
    count = lax.axis_size(axis)
    return lax.ppermute(array, axis, [(i, i ^ step) for i in range(count)])


def struct(*shape, dtype=F32):
    return jax.ShapeDtypeStruct(shape, dtype)


def params(mib):
    return pltpu.CompilerParams(vmem_limit_bytes=mib << 20)


def cost(flops, size):
    return pl.CostEstimate(flops=int(flops), bytes_accessed=int(size), transcendentals=0)


def body(memory_rows, list_owner, list_slot, pq_codes, valid_rows, centroids, codebook):
    row_count, width = memory_rows.shape
    lists = centroids.shape[0]
    subs, code_count, width_sub = codebook.shape
    owners, replicas = lax.axis_size("list"), lax.axis_size("rep")
    capacity = max(128, 4 * row_count // owners)
    group_subs = subs // replicas
    half = group_subs // 2
    padded = width_sub + 8
    book = jnp.transpose(codebook, (0, 2, 1))
    codes = pq_codes.T

    requests, position = pl.pallas_call(
        functools.partial(pack_kernel, owners, capacity),
        in_specs=[SMEM] + [VMEM] * 3,
        out_specs=[VMEM] * 2,
        out_shape=[
            struct(owners, subs + extra, capacity, dtype=BF16),
            struct(1, row_count, dtype=I32),
        ],
        compiler_params=params(60),
        cost_estimate=cost(1000, 1000),
        name="pack",
    )(
        valid_rows,
        list_owner.reshape(1, row_count),
        list_slot.reshape(1, row_count),
        codes,
    )
    requests = lax.all_to_all(requests, "list", 0, 0, tiled=True)

    row_sums = pl.pallas_call(
        row_sums_kernel,
        in_specs=[SMEM] + [VMEM] * 2,
        out_specs=VMEM,
        out_shape=struct(subs, padded, code_count),
        compiler_params=params(24),
        cost_estimate=cost(8 << 30, 16 << 20),
        name="row_sums",
    )(valid_rows, memory_rows, codes)
    offsets = pl.pallas_call(
        offset_kernel,
        in_specs=[VMEM] * 3,
        out_specs=VMEM,
        out_shape=struct(row_count, width),
        compiler_params=params(48),
        cost_estimate=cost(1000, 1000),
        name="offsets",
    )(memory_rows, codes, book)
    requests, row_sums = lax.optimization_barrier((requests, row_sums))
    gathered = pl.pallas_call(
        functools.partial(gather_kernel, subs),
        in_specs=[VMEM, HBM],
        out_specs=HBM,
        out_shape=struct(owners, capacity, width, dtype=BF16),
        scratch_shapes=[
            pltpu.VMEM((lists, width), BF16),
            pltpu.VMEM((owners, capacity, width), BF16),
            pltpu.SemaphoreType.DMA((4,)),
            pltpu.SemaphoreType.DMA((2,)),
        ],
        compiler_params=params(57),
        cost_estimate=cost(4 << 30, 6 << 20),
        name="gather",
    )(requests, centroids)
    pieces = lax.all_to_all(gathered, "list", 0, 0, tiled=True)

    half_shape = struct(replicas, half, padded, code_count)
    keep, send = pl.pallas_call(
        functools.partial(sums_kernel, replicas),
        in_specs=[VMEM] * 3,
        out_specs=[VMEM] * 2,
        out_shape=[half_shape] * 2,
        compiler_params=params(20),
        cost_estimate=cost(1000, 1000),
        name="sums",
    )(requests, gathered.reshape(owners * capacity, width), row_sums)

    own = keep + swap(send, "list", 1)
    row = lax.broadcasted_iota(I32, own.shape, 2)
    high = jnp.floor(own * (1.0 / 256.0))
    own = jnp.where(
        row < width_sub, own, jnp.where(row == width_sub, high, own - 256.0 * high)
    )
    parts = [own[0]] + [swap(own[s].astype(BF16), "rep", s) for s in range(1, replicas)]
    own = pl.pallas_call(
        functools.partial(encode_kernel, width_sub),
        in_specs=[VMEM] * replicas,
        out_specs=VMEM,
        out_shape=struct(half, padded, code_count, dtype=jnp.int16),
        compiler_params=params(20),
        cost_estimate=cost(1000, 1000),
        name="encode",
    )(*parts)
    own, offsets = lax.optimization_barrier((own, offsets))
    others = [swap(own, "list", s) for s in range(2, owners, 2)]
    row_error = pl.pallas_call(
        error_kernel,
        in_specs=[SMEM] + [VMEM] * 3,
        out_specs=VMEM,
        out_shape=struct(1, row_count),
        compiler_params=params(48),
        cost_estimate=cost(1000, 1000),
        name="errors",
    )(valid_rows, position, offsets, pieces.reshape(owners * capacity, width))
    row_error, *others = lax.optimization_barrier((row_error, *others))
    core = lax.axis_index("list") % 2
    start = lax.axis_index("rep") * group_subs + core * half
    prior = prior_weight * lax.dynamic_slice_in_dim(book, start, half, 0)
    parts = [part.astype(F32) for part in (own, *others)]
    parts = [
        jnp.where(
            lax.broadcasted_iota(I32, part.shape, 1) < width_sub,
            part * (jnp.exp2(part[:, width_sub + 2 : width_sub + 3]) / 16384.0),
            part,
        )
        for part in parts
    ]
    sums, high, low = (
        functools.reduce(jnp.add, [part[:, first:last] for part in parts])
        for first, last in (
            (0, width_sub),
            (width_sub, width_sub + 1),
            (width_sub + 1, width_sub + 2),
        )
    )
    own = (sums + prior) / (256.0 * high + low + prior_weight)
    other = swap(own, "list", 1)
    new_codebook = jnp.concatenate(
        [jnp.where(core == 0, own, other), jnp.where(core == 0, other, own)], axis=0
    )
    return (jnp.transpose(new_codebook, (0, 2, 1)), row_error.reshape(row_count))


def solution(mesh):
    in_specs = (
        P(("list", "rep"), None),
        P(("list", "rep"), None),
        P(("list", "rep")),
        P(("list", "rep"), None),
        P(("list", "rep")),
        P("list", None),
        P(),
    )
    out_specs = (P("rep", None, None), P(("list", "rep")))
    return jax.shard_map(body, mesh=mesh, in_specs=in_specs, out_specs=out_specs, check_vma=False)
```

```python
import functools

import jax
import jax.numpy as jnp
from jax import lax
from jax.experimental import pallas as pl
from jax.experimental.pallas import tpu as pltpu
from jax.sharding import PartitionSpec as P

prior_weight = 4.0
F32, BF16, I32 = jnp.float32, jnp.bfloat16, jnp.int32
VMEM = pl.BlockSpec(memory_space=pltpu.VMEM)
HBM = pl.BlockSpec(memory_space=pltpu.HBM)
SMEM = pl.BlockSpec(memory_space=pltpu.SMEM)
NT = (((1,), (1,)), ((), ()))
extra = 16


def mask_bf16(mask):
    return jnp.where(mask, 1.0, 0.0).astype(BF16)


def dot(a, b):
    return jnp.dot(a, b, preferred_element_type=F32)


def dot_nt(a, b):
    return lax.dot_general(a, b, NT, preferred_element_type=F32)


def pack_kernel(owners, capacity, valid, owner, slot, codes, requests, position_out):
    row_count = owner.shape[1]
    lane = lax.broadcasted_iota(I32, (1, row_count), 1)
    live = lane < valid[0]
    target = jnp.where(live, owner[...], -1)
    hit = jnp.where(lax.broadcasted_iota(I32, (owners, row_count), 0) == target, 1.0, 0.0)
    earlier = mask_bf16(
        lax.broadcasted_iota(I32, (row_count, row_count), 0)
        < lax.broadcasted_iota(I32, (row_count, row_count), 1)
    )
    before = dot(hit.astype(BF16), earlier)
    rank = jnp.sum(hit * before, axis=0, keepdims=True).astype(I32)
    position = jnp.where(live, target * capacity + rank, -1)
    position_out[...] = position

    high = (slot[...] // 256).astype(F32)
    low = (slot[...] % 256).astype(F32)
    which = lax.broadcasted_iota(I32, (extra, row_count), 0)
    tail = jnp.where(which == 0, high, jnp.where(which == 1, low, 0.0))
    info = jnp.concatenate([codes[...].astype(F32) - 256.0, tail], axis=0).astype(BF16)
    within = lax.broadcasted_iota(I32, (capacity, row_count), 0)
    for dest in range(owners):
        place_at = mask_bf16(within == position - dest * capacity)
        requests[dest] = dot_nt(info, place_at).astype(BF16)


def row_sums_kernel(valid, rows, codes, centres, out, held, loaded):
    load = pltpu.make_async_copy(centres.at[pl.ds(0, held.shape[0])], held, loaded)
    load.start()
    subs, padded, code_count = out.shape
    row_count, width = rows.shape
    width_sub = width // subs
    lane = lax.broadcasted_iota(I32, (1, row_count), 1)
    live_codes = jnp.where(lane < valid[0], codes[...], -1)
    columns = rows[...].T
    code_iota = lax.broadcasted_iota(I32, (code_count, row_count), 0)
    ones = jnp.ones((16, row_count), BF16)
    for m in range(subs):
        code_hit = mask_bf16(code_iota == live_codes[m : m + 1])
        out[m, 0:width_sub] = dot_nt(columns[m * width_sub : (m + 1) * width_sub], code_hit)
        out[m, width_sub:padded] = dot_nt(ones, code_hit)[0 : padded - width_sub]
    load.wait()


def sums_kernel(replicas, requests, gathered, row_sums, keep, send):
    subs, padded, code_count = row_sums.shape
    owners, _, capacity = requests.shape
    slots, width = gathered.shape
    width_sub = width // subs
    group_subs = subs // replicas
    half = group_subs // 2
    mine = jnp.bitwise_and(lax.axis_index("list"), 1)
    rep = lax.axis_index("rep")
    asked = jnp.concatenate([requests[j] for j in range(owners)], axis=1)
    codes = asked.astype(F32).astype(I32) + 256
    code_iota = lax.broadcasted_iota(I32, (code_count, slots), 0)
    first = lax.broadcasted_iota(I32, (code_count, 2 * width_sub), 1) < width_sub
    for pair in range(subs // 2):
        span = slice(pair * 2 * width_sub, (pair + 1) * 2 * width_sub)
        found = [
            dot(mask_bf16(code_iota == codes[m : m + 1]), gathered[:, span])
            for m in (2 * pair, 2 * pair + 1)
        ]
        centre_sums = jnp.where(first, found[0], found[1]).T
        for j in range(2):
            m = 2 * pair + j
            sums = row_sums[m, 0:width_sub] - centre_sums[j * width_sub : (j + 1) * width_sub]
            counts = row_sums[m, width_sub:padded]
            group, at = m // group_subs, m % group_subs
            step = jnp.bitwise_xor(rep, group)

            def store(out, sums=sums, counts=counts, step=step, at=at):
                out[step, at % half, 0:width_sub] = sums
                out[step, at % half, width_sub:padded] = counts

            pl.when(mine == at // half)(functools.partial(store, keep))
            pl.when(mine != at // half)(functools.partial(store, send))


def gather_kernel(subs, requests, held, centres, pieces, near, found, loaded, written):
    owners, _, capacity = requests.shape
    lists = centres.shape[0]
    ready = held.shape[0]
    parts, chunks = loaded.shape[0], written.shape[0]
    chunk = owners // chunks
    span = chunk * capacity
    step = (lists - ready) // parts
    loads, stores = [], []
    for part in range(parts):
        load = pltpu.make_async_copy(
            centres.at[pl.ds(ready + part * step, step)],
            near.at[pl.ds(part * step, step)],
            loaded.at[part],
        )
        load.start()
        loads.append(load)
    for index in range(chunks):
        asked = jnp.concatenate([requests[index * chunk + j] for j in range(chunk)], axis=1)
        turned = asked.astype(F32).T.astype(I32)
        high, low = (turned[:, subs + i : subs + i + 1] for i in range(2))
        low_hit = mask_bf16(lax.broadcasted_iota(I32, (span, 256), 1) == low)
        hits = [low_hit * mask_bf16(high == h) for h in range(lists // 256)]
        total = dot(jnp.concatenate(hits[: ready // 256], axis=1), held[...])
        for part in range(parts):
            first, last = part * step, (part + 1) * step
            hit = jnp.concatenate(hits[(ready + first) // 256 : (ready + last) // 256], axis=1)
            if index == 0:
                loads[part].wait()
            total += dot(hit, near[first:last])
        block = pl.ds(index * chunk, chunk)
        found[block] = total.astype(BF16).reshape((chunk, *found.shape[1:]))
        stores.append(
            pltpu.make_async_copy(found.at[block], pieces.at[block], written.at[index])
        )
        stores[-1].start()
    for store in stores:
        store.wait()


def offset_kernel(rows, codes, book, out):
    subs, width_sub, code_count = book.shape
    row_count = rows.shape[0]
    turned = codes[...].astype(F32).T.astype(I32)
    code_iota = lax.broadcasted_iota(I32, (row_count, code_count), 1)
    empty = jnp.zeros((width_sub, code_count), BF16)
    for pair in range(subs // 2):
        hits, highs, lows = [], [], []
        for m in (2 * pair, 2 * pair + 1):
            hits.append(mask_bf16(code_iota == turned[:, m : m + 1]))
            high = book[m].astype(BF16)
            highs.append(high)
            lows.append((book[m] - high.astype(F32)).astype(BF16))
        table = jnp.concatenate(
            [
                jnp.concatenate([highs[0], empty], axis=1),
                jnp.concatenate([empty, highs[1]], axis=1),
                jnp.concatenate([lows[0], empty], axis=1),
                jnp.concatenate([empty, lows[1]], axis=1),
            ],
            axis=0,
        )
        recon = dot_nt(jnp.concatenate(hits, axis=1), table)
        lanes = 2 * width_sub
        span = slice(pair * lanes, (pair + 1) * lanes)
        out[:, span] = rows[:, span].astype(F32) - (recon[:, :lanes] + recon[:, lanes:])


def error_kernel(valid, position, offsets, centres, out):
    slots, width = centres.shape
    row_count = offsets.shape[0]
    column_at = jnp.broadcast_to(position[...].astype(F32), (8, row_count)).T.astype(I32)[:, 0:1]
    hit = mask_bf16(lax.broadcasted_iota(I32, (row_count, slots), 1) == column_at)
    partial = jnp.zeros((row_count, 128), F32)
    for start in range(0, width, 256):
        gap = offsets[:, start : start + 256] - dot(hit, centres[:, start : start + 256])
        square = gap * gap
        partial += square[:, :128] + square[:, 128:]
    error = jnp.sum(partial.T, axis=0, keepdims=True) * (1.0 / width)
    lane = lax.broadcasted_iota(I32, (1, row_count), 1)
    out[...] = jnp.where(lane < valid[0], error, 0.0)


def encode_kernel(width_sub, book, *refs):
    parts = refs[:-3]
    out, near, loaded = refs[-3:]
    half, padded, code_count = out.shape
    me, rep = lax.axis_index("list"), lax.axis_index("rep")
    start = (2 * rep + jnp.bitwise_and(me, 1)) * half
    load = pltpu.make_async_copy(book.at[pl.ds(start, half)], near, loaded)
    load.start()
    prior = jnp.where(me < 2, prior_weight, 0.0)
    which = lax.broadcasted_iota(I32, (padded - width_sub, code_count), 0)
    for m in range(half):
        total = parts[0][m]
        for part in parts[1:]:
            total += part[m].astype(F32)
        if m == 0:
            load.wait()
        sums = total[:width_sub] + prior * near[m]
        counts = total[width_sub:] + jnp.where(which == 1, prior, 0.0)
        top = jnp.max(jnp.abs(sums), axis=0, keepdims=True)
        exponent = jnp.clip(jnp.ceil(jnp.log2(top)) - 1.0, -125.0, 127.0)
        scaled = jnp.clip(jnp.round(sums / jnp.exp2(exponent) * 16384.0), -32767.0, 32767.0)
        tail = jnp.where(which < 2, counts, jnp.where(which == 2, exponent, 0.0))
        out[m] = jnp.concatenate([scaled, tail], axis=0).astype(I32).astype(jnp.int16)


def swap(array, axis, step):
    count = lax.axis_size(axis)
    return lax.ppermute(array, axis, [(i, i ^ step) for i in range(count)])


def struct(*shape, dtype=F32):
    return jax.ShapeDtypeStruct(shape, dtype)


def params(mib):
    return pltpu.CompilerParams(vmem_limit_bytes=mib << 20)


def cost(flops, size):
    return pl.CostEstimate(flops=int(flops), bytes_accessed=int(size), transcendentals=0)


def body(memory_rows, list_owner, list_slot, pq_codes, valid_rows, centroids, codebook):
    row_count, width = memory_rows.shape
    lists = centroids.shape[0]
    subs, code_count, width_sub = codebook.shape
    owners, replicas = lax.axis_size("list"), lax.axis_size("rep")
    capacity = max(128, 4 * row_count // owners)
    group_subs = subs // replicas
    half = group_subs // 2
    padded = width_sub + 8
    book = jnp.transpose(codebook, (0, 2, 1))
    codes = pq_codes.T

    requests, position = pl.pallas_call(
        functools.partial(pack_kernel, owners, capacity),
        in_specs=[SMEM] + [VMEM] * 3,
        out_specs=[VMEM] * 2,
        out_shape=[
            struct(owners, subs + extra, capacity, dtype=BF16),
            struct(1, row_count, dtype=I32),
        ],
        compiler_params=params(60),
        cost_estimate=cost(1000, 1000),
        name="pack",
    )(
        valid_rows,
        list_owner.reshape(1, row_count),
        list_slot.reshape(1, row_count),
        codes,
    )
    requests = lax.all_to_all(requests, "list", 0, 0, tiled=True)

    far = pltpu.with_memory_space_constraint(centroids, pltpu.HBM)
    row_sums, held = pl.pallas_call(
        row_sums_kernel,
        in_specs=[SMEM] + [VMEM] * 2 + [HBM],
        out_specs=[VMEM] * 2,
        out_shape=[
            struct(subs, padded, code_count),
            struct(lists // 2, width, dtype=BF16),
        ],
        scratch_shapes=[pltpu.SemaphoreType.DMA],
        compiler_params=params(24),
        cost_estimate=cost(2 << 30, 4 << 20),
        name="row_sums",
    )(valid_rows, memory_rows, codes, far)
    offsets = pl.pallas_call(
        offset_kernel,
        in_specs=[VMEM] * 3,
        out_specs=VMEM,
        out_shape=struct(row_count, width),
        compiler_params=params(48),
        cost_estimate=cost(1000, 1000),
        name="offsets",
    )(memory_rows, codes, book)
    gathered = pl.pallas_call(
        functools.partial(gather_kernel, subs),
        in_specs=[VMEM, VMEM, HBM],
        out_specs=HBM,
        out_shape=pltpu.HBM((owners, capacity, width), BF16),
        scratch_shapes=[
            pltpu.VMEM((lists - lists // 2, width), BF16),
            pltpu.VMEM((owners, capacity, width), BF16),
            pltpu.SemaphoreType.DMA((4,)),
            pltpu.SemaphoreType.DMA((2,)),
        ],
        compiler_params=params(20 + 5 * (owners * capacity * width >> 19)),
        cost_estimate=cost(4 << 30, 6 << 20),
        name="gather",
    )(requests, held, far)
    pieces = lax.all_to_all(gathered, "list", 0, 0, tiled=True)

    half_shape = struct(replicas, half, padded, code_count)
    keep, send = pl.pallas_call(
        functools.partial(sums_kernel, replicas),
        in_specs=[VMEM] * 3,
        out_specs=[VMEM] * 2,
        out_shape=[half_shape] * 2,
        compiler_params=params(20),
        cost_estimate=cost(1000, 1000),
        name="sums",
    )(requests, gathered.reshape(owners * capacity, width), row_sums)

    own = keep + swap(send, "list", 1)
    row = lax.broadcasted_iota(I32, own.shape, 2)
    high = jnp.floor(own * (1.0 / 256.0))
    own = jnp.where(
        row < width_sub, own, jnp.where(row == width_sub, high, own - 256.0 * high)
    )
    parts = [own[0]] + [swap(own[s].astype(BF16), "rep", s) for s in range(1, replicas)]
    own = pl.pallas_call(
        functools.partial(encode_kernel, width_sub),
        in_specs=[HBM] + [VMEM] * replicas,
        out_specs=VMEM,
        out_shape=struct(half, padded, code_count, dtype=jnp.int16),
        scratch_shapes=[
            pltpu.VMEM((half, width_sub, code_count), F32),
            pltpu.SemaphoreType.DMA,
        ],
        compiler_params=params(20),
        cost_estimate=cost(1000, 1000),
        name="encode",
    )(book, *parts)
    own, offsets = lax.optimization_barrier((own, offsets))
    others = [swap(own, "list", s) for s in range(2, owners, 2)]
    row_error = pl.pallas_call(
        error_kernel,
        in_specs=[SMEM] + [VMEM] * 3,
        out_specs=VMEM,
        out_shape=struct(1, row_count),
        compiler_params=params(48),
        cost_estimate=cost(1000, 1000),
        name="errors",
    )(valid_rows, position, offsets, pieces.reshape(owners * capacity, width))
    row_error, *others = lax.optimization_barrier((row_error, *others))
    core = lax.axis_index("list") % 2
    parts = [part.astype(F32) for part in (own, *others)]
    parts = [
        jnp.where(
            lax.broadcasted_iota(I32, part.shape, 1) < width_sub,
            part * (jnp.exp2(part[:, width_sub + 2 : width_sub + 3]) / 16384.0),
            part,
        )
        for part in parts
    ]
    sums, high, low = (
        functools.reduce(jnp.add, [part[:, first:last] for part in parts])
        for first, last in (
            (0, width_sub),
            (width_sub, width_sub + 1),
            (width_sub + 1, width_sub + 2),
        )
    )
    own = sums / (256.0 * high + low)
    other = swap(own, "list", 1)
    new_codebook = jnp.concatenate(
        [jnp.where(core == 0, own, other), jnp.where(core == 0, other, own)], axis=0
    )
    return (jnp.transpose(new_codebook, (0, 2, 1)), row_error.reshape(row_count))


def solution(mesh):
    in_specs = (
        P(("list", "rep"), None),
        P(("list", "rep"), None),
        P(("list", "rep")),
        P(("list", "rep"), None),
        P(("list", "rep")),
        P("list", None),
        P(),
    )
    out_specs = (P("rep", None, None), P(("list", "rep")))
    return jax.shard_map(body, mesh=mesh, in_specs=in_specs, out_specs=out_specs, check_vma=False)
```

```python
import functools

import jax
import jax.numpy as jnp
from jax import lax
from jax.experimental import pallas as pl
from jax.experimental.pallas import tpu as pltpu
from jax.sharding import PartitionSpec as P

prior_weight = 4.0
F32, BF16, I32 = jnp.float32, jnp.bfloat16, jnp.int32
VMEM = pl.BlockSpec(memory_space=pltpu.VMEM)
HBM = pl.BlockSpec(memory_space=pltpu.HBM)
SMEM = pl.BlockSpec(memory_space=pltpu.SMEM)
NT = (((1,), (1,)), ((), ()))
extra = 16


def mask_bf16(mask):
    return jnp.where(mask, 1.0, 0.0).astype(BF16)


def dot(a, b):
    return jnp.dot(a, b, preferred_element_type=F32)


def dot_nt(a, b):
    return lax.dot_general(a, b, NT, preferred_element_type=F32)


def pack_kernel(owners, capacity, valid, owner, slot, codes, requests, position_out):
    row_count = owner.shape[1]
    lane = lax.broadcasted_iota(I32, (1, row_count), 1)
    live = lane < valid[0]
    target = jnp.where(live, owner[...], -1)
    hit = jnp.where(lax.broadcasted_iota(I32, (owners, row_count), 0) == target, 1.0, 0.0)
    earlier = mask_bf16(
        lax.broadcasted_iota(I32, (row_count, row_count), 0)
        < lax.broadcasted_iota(I32, (row_count, row_count), 1)
    )
    before = dot(hit.astype(BF16), earlier)
    rank = jnp.sum(hit * before, axis=0, keepdims=True).astype(I32)
    position = jnp.where(live, target * capacity + rank, -1)
    position_out[...] = position

    high = (slot[...] // 256).astype(F32)
    low = (slot[...] % 256).astype(F32)
    which = lax.broadcasted_iota(I32, (extra, row_count), 0)
    tail = jnp.where(which == 0, high, jnp.where(which == 1, low, 0.0))
    info = jnp.concatenate([codes[...].astype(F32) - 256.0, tail], axis=0).astype(BF16)
    within = lax.broadcasted_iota(I32, (capacity, row_count), 0)
    for dest in range(owners):
        place_at = mask_bf16(within == position - dest * capacity)
        requests[dest] = dot_nt(info, place_at).astype(BF16)


def row_sums_kernel(valid, rows, codes, centres, out, held, loaded):
    load = pltpu.make_async_copy(centres.at[pl.ds(0, held.shape[0])], held, loaded)
    load.start()
    subs, padded, code_count = out.shape
    row_count, width = rows.shape
    width_sub = width // subs
    lane = lax.broadcasted_iota(I32, (1, row_count), 1)
    live_codes = jnp.where(lane < valid[0], codes[...], -1)
    columns = rows[...].T
    code_iota = lax.broadcasted_iota(I32, (code_count, row_count), 0)
    ones = jnp.ones((16, row_count), BF16)
    for m in range(subs):
        code_hit = mask_bf16(code_iota == live_codes[m : m + 1])
        out[m, 0:width_sub] = dot_nt(columns[m * width_sub : (m + 1) * width_sub], code_hit)
        out[m, width_sub:padded] = dot_nt(ones, code_hit)[0 : padded - width_sub]
    load.wait()


def sums_kernel(replicas, requests, gathered, row_sums, keep, send):
    subs, padded, code_count = row_sums.shape
    owners, _, capacity = requests.shape
    slots, width = gathered.shape
    width_sub = width // subs
    group_subs = subs // replicas
    half = group_subs // 2
    mine = jnp.bitwise_and(lax.axis_index("list"), 1)
    rep = lax.axis_index("rep")
    asked = jnp.concatenate([requests[j] for j in range(owners)], axis=1)
    codes = asked.astype(F32).astype(I32) + 256
    code_iota = lax.broadcasted_iota(I32, (code_count, slots), 0)
    first = lax.broadcasted_iota(I32, (code_count, 2 * width_sub), 1) < width_sub
    for pair in range(subs // 2):
        span = slice(pair * 2 * width_sub, (pair + 1) * 2 * width_sub)
        found = [
            dot(mask_bf16(code_iota == codes[m : m + 1]), gathered[:, span])
            for m in (2 * pair, 2 * pair + 1)
        ]
        centre_sums = jnp.where(first, found[0], found[1]).T
        for j in range(2):
            m = 2 * pair + j
            sums = row_sums[m, 0:width_sub] - centre_sums[j * width_sub : (j + 1) * width_sub]
            counts = row_sums[m, width_sub:padded]
            group, at = m // group_subs, m % group_subs
            step = jnp.bitwise_xor(rep, group)

            def store(out, sums=sums, counts=counts, step=step, at=at):
                out[step, at % half, 0:width_sub] = sums
                out[step, at % half, width_sub:padded] = counts

            pl.when(mine == at // half)(functools.partial(store, keep))
            pl.when(mine != at // half)(functools.partial(store, send))


def gather_kernel(subs, requests, held, centres, pieces, near, found, loaded, written):
    owners, _, capacity = requests.shape
    lists = centres.shape[0]
    ready = held.shape[0]
    parts, chunks = loaded.shape[0], written.shape[0]
    chunk = owners // chunks
    span = chunk * capacity
    step = (lists - ready) // parts
    loads, stores = [], []
    for part in range(parts):
        load = pltpu.make_async_copy(
            centres.at[pl.ds(ready + part * step, step)],
            near.at[pl.ds(part * step, step)],
            loaded.at[part],
        )
        load.start()
        loads.append(load)
    for index in range(chunks):
        asked = jnp.concatenate([requests[index * chunk + j] for j in range(chunk)], axis=1)
        turned = asked.astype(F32).T.astype(I32)
        high, low = (turned[:, subs + i : subs + i + 1] for i in range(2))
        low_hit = mask_bf16(lax.broadcasted_iota(I32, (span, 256), 1) == low)
        hits = [low_hit * mask_bf16(high == h) for h in range(lists // 256)]
        total = dot(jnp.concatenate(hits[: ready // 256], axis=1), held[...])
        for part in range(parts):
            first, last = part * step, (part + 1) * step
            hit = jnp.concatenate(hits[(ready + first) // 256 : (ready + last) // 256], axis=1)
            if index == 0:
                loads[part].wait()
            total += dot(hit, near[first:last])
        block = pl.ds(index * chunk, chunk)
        found[block] = total.astype(BF16).reshape((chunk, *found.shape[1:]))
        stores.append(
            pltpu.make_async_copy(found.at[block], pieces.at[block], written.at[index])
        )
        stores[-1].start()
    for store in stores:
        store.wait()


def offset_kernel(rows, codes, book, out):
    subs, width_sub, code_count = book.shape
    row_count = rows.shape[0]
    turned = codes[...].astype(F32).T.astype(I32)
    code_iota = lax.broadcasted_iota(I32, (row_count, code_count), 1)
    empty = jnp.zeros((width_sub, code_count), BF16)
    for pair in range(subs // 2):
        hits, highs, lows = [], [], []
        for m in (2 * pair, 2 * pair + 1):
            hits.append(mask_bf16(code_iota == turned[:, m : m + 1]))
            high = book[m].astype(BF16)
            highs.append(high)
            lows.append((book[m] - high.astype(F32)).astype(BF16))
        table = jnp.concatenate(
            [
                jnp.concatenate([highs[0], empty], axis=1),
                jnp.concatenate([empty, highs[1]], axis=1),
                jnp.concatenate([lows[0], empty], axis=1),
                jnp.concatenate([empty, lows[1]], axis=1),
            ],
            axis=0,
        )
        recon = dot_nt(jnp.concatenate(hits, axis=1), table)
        lanes = 2 * width_sub
        span = slice(pair * lanes, (pair + 1) * lanes)
        out[:, span] = rows[:, span].astype(F32) - (recon[:, :lanes] + recon[:, lanes:])


def error_kernel(valid, position, offsets, centres, out):
    slots, width = centres.shape
    row_count = offsets.shape[0]
    column_at = jnp.broadcast_to(position[...].astype(F32), (8, row_count)).T.astype(I32)[:, 0:1]
    hit = mask_bf16(lax.broadcasted_iota(I32, (row_count, slots), 1) == column_at)
    partial = jnp.zeros((row_count, 128), F32)
    for start in range(0, width, 256):
        gap = offsets[:, start : start + 256] - dot(hit, centres[:, start : start + 256])
        square = gap * gap
        partial += square[:, :128] + square[:, 128:]
    error = jnp.sum(partial.T, axis=0, keepdims=True) * (1.0 / width)
    lane = lax.broadcasted_iota(I32, (1, row_count), 1)
    out[...] = jnp.where(lane < valid[0], error, 0.0)


def scaled_codes(sums, counts, which):
    top = jnp.max(jnp.abs(sums), axis=0, keepdims=True)
    exponent = jnp.clip(jnp.ceil(jnp.log2(top)) - 1.0, -125.0, 127.0)
    scaled = jnp.clip(jnp.round(sums / jnp.exp2(exponent) * 16384.0), -32767.0, 32767.0)
    tail = jnp.where(which < 2, counts, jnp.where(which == 2, exponent, 0.0))
    return jnp.concatenate([scaled, tail], axis=0).astype(I32).astype(jnp.int16)


def add_kernel(width_sub, keep, got, own, *codes):
    replicas, half, padded, code_count = keep.shape
    which = lax.broadcasted_iota(I32, (padded - width_sub, code_count), 0)
    for step in range(replicas):
        for m in range(half):
            sums = keep[step, m, 0:width_sub] + got[step, m, 0:width_sub]
            counts = keep[step, m, width_sub:padded] + got[step, m, width_sub:padded]
            high = jnp.floor(counts * (1.0 / 256.0))
            counts = jnp.where(which == 0, high, counts - 256.0 * high)
            if step == 0:
                own[m, 0:width_sub] = sums
                own[m, width_sub:padded] = counts
            else:
                codes[step - 1][m] = scaled_codes(sums, counts, which)


def encode_kernel(width_sub, book, own, *refs):
    parts = refs[:-3]
    out, near, loaded = refs[-3:]
    half, padded, code_count = out.shape
    me, rep = lax.axis_index("list"), lax.axis_index("rep")
    start = (2 * rep + jnp.bitwise_and(me, 1)) * half
    load = pltpu.make_async_copy(book.at[pl.ds(start, half)], near, loaded)
    load.start()
    prior = jnp.where(me < 2, prior_weight, 0.0)
    which = lax.broadcasted_iota(I32, (padded - width_sub, code_count), 0)
    load.wait()
    for m in range(half):
        sums = own[m, 0:width_sub] + prior * near[m]
        counts = own[m, width_sub:padded] + jnp.where(which == 1, prior, 0.0)
        for part in parts:
            coded = part[m].astype(I32).astype(F32)
            tail = coded[width_sub:padded]
            sums += coded[0:width_sub] * (jnp.exp2(tail[2:3]) * (1.0 / 16384.0))
            counts += tail
        out[m] = scaled_codes(sums, counts, which)


def swap(array, axis, step):
    count = lax.axis_size(axis)
    return lax.ppermute(array, axis, [(i, i ^ step) for i in range(count)])


def struct(*shape, dtype=F32):
    return jax.ShapeDtypeStruct(shape, dtype)


def params(mib):
    return pltpu.CompilerParams(vmem_limit_bytes=mib << 20)


def cost(flops, size):
    return pl.CostEstimate(flops=int(flops), bytes_accessed=int(size), transcendentals=0)


def body(memory_rows, list_owner, list_slot, pq_codes, valid_rows, centroids, codebook):
    row_count, width = memory_rows.shape
    lists = centroids.shape[0]
    subs, code_count, width_sub = codebook.shape
    owners, replicas = lax.axis_size("list"), lax.axis_size("rep")
    capacity = max(128, 4 * row_count // owners)
    group_subs = subs // replicas
    half = group_subs // 2
    padded = width_sub + 8
    book = jnp.transpose(codebook, (0, 2, 1))
    codes = pq_codes.T

    requests, position = pl.pallas_call(
        functools.partial(pack_kernel, owners, capacity),
        in_specs=[SMEM] + [VMEM] * 3,
        out_specs=[VMEM] * 2,
        out_shape=[
            struct(owners, subs + extra, capacity, dtype=BF16),
            struct(1, row_count, dtype=I32),
        ],
        compiler_params=params(60),
        cost_estimate=cost(1000, 1000),
        name="pack",
    )(
        valid_rows,
        list_owner.reshape(1, row_count),
        list_slot.reshape(1, row_count),
        codes,
    )
    requests = lax.all_to_all(requests, "list", 0, 0, tiled=True)

    far, far_rows, far_codes = (
        pltpu.with_memory_space_constraint(array, pltpu.HBM)
        for array in (centroids, memory_rows, codes)
    )
    row_sums, held = pl.pallas_call(
        row_sums_kernel,
        in_specs=[SMEM] + [VMEM] * 2 + [HBM],
        out_specs=[VMEM] * 2,
        out_shape=[
            struct(subs, padded, code_count),
            struct(lists // 2, width, dtype=BF16),
        ],
        scratch_shapes=[pltpu.SemaphoreType.DMA],
        compiler_params=params(24),
        cost_estimate=cost(2 << 30, 4 << 20),
        name="row_sums",
    )(valid_rows, far_rows, far_codes, far)
    offsets = pl.pallas_call(
        offset_kernel,
        in_specs=[VMEM] * 3,
        out_specs=VMEM,
        out_shape=struct(row_count, width),
        compiler_params=params(48),
        cost_estimate=cost(1000, 1000),
        name="offsets",
    )(memory_rows, codes, book)
    gathered = pl.pallas_call(
        functools.partial(gather_kernel, subs),
        in_specs=[VMEM, VMEM, HBM],
        out_specs=HBM,
        out_shape=pltpu.HBM((owners, capacity, width), BF16),
        scratch_shapes=[
            pltpu.VMEM((lists - lists // 2, width), BF16),
            pltpu.VMEM((owners, capacity, width), BF16),
            pltpu.SemaphoreType.DMA((4,)),
            pltpu.SemaphoreType.DMA((2,)),
        ],
        compiler_params=params(20 + 5 * (owners * capacity * width >> 19)),
        cost_estimate=cost(4 << 30, 6 << 20),
        name="gather",
    )(requests, held, far)
    pieces = lax.all_to_all(gathered, "list", 0, 0, tiled=True)

    half_shape = struct(replicas, half, padded, code_count)
    keep, send = pl.pallas_call(
        functools.partial(sums_kernel, replicas),
        in_specs=[VMEM] * 3,
        out_specs=[VMEM] * 2,
        out_shape=[half_shape] * 2,
        compiler_params=params(20),
        cost_estimate=cost(1000, 1000),
        name="sums",
    )(requests, gathered.reshape(owners * capacity, width), row_sums)

    part_shape = (half, padded, code_count)
    own, *codes_out = pl.pallas_call(
        functools.partial(add_kernel, width_sub),
        in_specs=[VMEM] * 2,
        out_specs=[VMEM] * replicas,
        out_shape=[struct(*part_shape)]
        + [struct(*part_shape, dtype=jnp.int16)] * (replicas - 1),
        compiler_params=params(20),
        cost_estimate=cost(1000, 1000),
        name="add",
    )(keep, swap(send, "list", 1))
    parts = [own] + [swap(codes_out[s - 1], "rep", s) for s in range(1, replicas)]
    own = pl.pallas_call(
        functools.partial(encode_kernel, width_sub),
        in_specs=[HBM] + [VMEM] * replicas,
        out_specs=VMEM,
        out_shape=struct(half, padded, code_count, dtype=jnp.int16),
        scratch_shapes=[
            pltpu.VMEM((half, width_sub, code_count), F32),
            pltpu.SemaphoreType.DMA,
        ],
        compiler_params=params(20),
        cost_estimate=cost(1000, 1000),
        name="encode",
    )(book, *parts)
    own, offsets = lax.optimization_barrier((own, offsets))
    others = [swap(own, "list", s) for s in range(2, owners, 2)]
    row_error = pl.pallas_call(
        error_kernel,
        in_specs=[SMEM] + [VMEM] * 3,
        out_specs=VMEM,
        out_shape=struct(1, row_count),
        compiler_params=params(48),
        cost_estimate=cost(1000, 1000),
        name="errors",
    )(valid_rows, position, offsets, pieces.reshape(owners * capacity, width))
    row_error, *others = lax.optimization_barrier((row_error, *others))
    core = lax.axis_index("list") % 2
    parts = [part.astype(F32) for part in (own, *others)]
    parts = [
        jnp.where(
            lax.broadcasted_iota(I32, part.shape, 1) < width_sub,
            part * (jnp.exp2(part[:, width_sub + 2 : width_sub + 3]) / 16384.0),
            part,
        )
        for part in parts
    ]
    sums, high, low = (
        functools.reduce(jnp.add, [part[:, first:last] for part in parts])
        for first, last in (
            (0, width_sub),
            (width_sub, width_sub + 1),
            (width_sub + 1, width_sub + 2),
        )
    )
    own = sums / (256.0 * high + low)
    other = swap(own, "list", 1)
    new_codebook = jnp.concatenate(
        [jnp.where(core == 0, own, other), jnp.where(core == 0, other, own)], axis=0
    )
    return (jnp.transpose(new_codebook, (0, 2, 1)), row_error.reshape(row_count))


def solution(mesh):
    in_specs = (
        P(("list", "rep"), None),
        P(("list", "rep"), None),
        P(("list", "rep")),
        P(("list", "rep"), None),
        P(("list", "rep")),
        P("list", None),
        P(),
    )
    out_specs = (P("rep", None, None), P(("list", "rep")))
    return jax.shard_map(body, mesh=mesh, in_specs=in_specs, out_specs=out_specs, check_vma=False)
```

```python
import functools

import jax
import jax.numpy as jnp
from jax import lax
from jax.experimental import pallas as pl
from jax.experimental.pallas import tpu as pltpu
from jax.sharding import PartitionSpec as P

prior_weight = 4.0
F32, BF16, I32 = jnp.float32, jnp.bfloat16, jnp.int32
VMEM = pl.BlockSpec(memory_space=pltpu.VMEM)
HBM = pl.BlockSpec(memory_space=pltpu.HBM)
SMEM = pl.BlockSpec(memory_space=pltpu.SMEM)
NT = (((1,), (1,)), ((), ()))
extra = 16


def mask_bf16(mask):
    return jnp.where(mask, 1.0, 0.0).astype(BF16)


def dot(a, b):
    return jnp.dot(a, b, preferred_element_type=F32)


def dot_nt(a, b):
    return lax.dot_general(a, b, NT, preferred_element_type=F32)


def pack_kernel(owners, capacity, valid, owner, slot, codes, requests, position_out):
    row_count = owner.shape[1]
    lane = lax.broadcasted_iota(I32, (1, row_count), 1)
    live = lane < valid[0]
    target = jnp.where(live, owner[...], -1)
    hit = jnp.where(lax.broadcasted_iota(I32, (owners, row_count), 0) == target, 1.0, 0.0)
    earlier = mask_bf16(
        lax.broadcasted_iota(I32, (row_count, row_count), 0)
        < lax.broadcasted_iota(I32, (row_count, row_count), 1)
    )
    before = dot(hit.astype(BF16), earlier)
    rank = jnp.sum(hit * before, axis=0, keepdims=True).astype(I32)
    position = jnp.where(live, target * capacity + rank, -1)
    position_out[...] = position

    high = (slot[...] // 256).astype(F32)
    low = (slot[...] % 256).astype(F32)
    which = lax.broadcasted_iota(I32, (extra, row_count), 0)
    tail = jnp.where(which == 0, high, jnp.where(which == 1, low, 0.0))
    info = jnp.concatenate([codes[...].astype(F32) - 256.0, tail], axis=0).astype(BF16)
    within = lax.broadcasted_iota(I32, (capacity, row_count), 0)
    for dest in range(owners):
        place_at = mask_bf16(within == position - dest * capacity)
        requests[dest] = dot_nt(info, place_at).astype(BF16)


def row_sums_kernel(valid, rows, codes, centres, out, held, loaded):
    load = pltpu.make_async_copy(centres.at[pl.ds(0, held.shape[0])], held, loaded)
    load.start()
    subs, padded, code_count = out.shape
    row_count, width = rows.shape
    width_sub = width // subs
    lane = lax.broadcasted_iota(I32, (1, row_count), 1)
    live_codes = jnp.where(lane < valid[0], codes[...], -1)
    columns = rows[...].T
    code_iota = lax.broadcasted_iota(I32, (code_count, row_count), 0)
    ones = jnp.ones((16, row_count), BF16)
    for m in range(subs):
        code_hit = mask_bf16(code_iota == live_codes[m : m + 1])
        out[m, 0:width_sub] = dot_nt(columns[m * width_sub : (m + 1) * width_sub], code_hit)
        out[m, width_sub:padded] = dot_nt(ones, code_hit)[0 : padded - width_sub]
    load.wait()


def sums_kernel(replicas, requests, gathered, row_sums, keep, send):
    subs, padded, code_count = row_sums.shape
    owners, _, capacity = requests.shape
    slots, width = gathered.shape
    width_sub = width // subs
    group_subs = subs // replicas
    half = group_subs // 2
    mine = jnp.bitwise_and(lax.axis_index("list"), 1)
    rep = lax.axis_index("rep")
    asked = jnp.concatenate([requests[j] for j in range(owners)], axis=1)
    codes = asked.astype(F32).astype(I32) + 256
    code_iota = lax.broadcasted_iota(I32, (code_count, slots), 0)
    first = lax.broadcasted_iota(I32, (code_count, 2 * width_sub), 1) < width_sub
    for pair in range(subs // 2):
        span = slice(pair * 2 * width_sub, (pair + 1) * 2 * width_sub)
        found = [
            dot(mask_bf16(code_iota == codes[m : m + 1]), gathered[:, span])
            for m in (2 * pair, 2 * pair + 1)
        ]
        centre_sums = jnp.where(first, found[0], found[1]).T
        for j in range(2):
            m = 2 * pair + j
            sums = row_sums[m, 0:width_sub] - centre_sums[j * width_sub : (j + 1) * width_sub]
            counts = row_sums[m, width_sub:padded]
            group, at = m // group_subs, m % group_subs
            step = jnp.bitwise_xor(rep, group)

            def store(out, sums=sums, counts=counts, step=step, at=at):
                out[step, at % half, 0:width_sub] = sums
                out[step, at % half, width_sub:padded] = counts

            pl.when(mine == at // half)(functools.partial(store, keep))
            pl.when(mine != at // half)(functools.partial(store, send))


def gather_kernel(subs, requests, held, centres, pieces, near, found, loaded, written):
    owners, _, capacity = requests.shape
    lists = centres.shape[0]
    ready = held.shape[0]
    parts, chunks = loaded.shape[0], written.shape[0]
    chunk = owners // chunks
    span = chunk * capacity
    step = (lists - ready) // parts
    loads, stores = [], []
    for part in range(parts):
        load = pltpu.make_async_copy(
            centres.at[pl.ds(ready + part * step, step)],
            near.at[pl.ds(part * step, step)],
            loaded.at[part],
        )
        load.start()
        loads.append(load)
    for index in range(chunks):
        asked = jnp.concatenate([requests[index * chunk + j] for j in range(chunk)], axis=1)
        turned = asked.astype(F32).T.astype(I32)
        high, low = (turned[:, subs + i : subs + i + 1] for i in range(2))
        low_hit = mask_bf16(lax.broadcasted_iota(I32, (span, 256), 1) == low)
        hits = [low_hit * mask_bf16(high == h) for h in range(lists // 256)]
        total = dot(jnp.concatenate(hits[: ready // 256], axis=1), held[...])
        for part in range(parts):
            first, last = part * step, (part + 1) * step
            hit = jnp.concatenate(hits[(ready + first) // 256 : (ready + last) // 256], axis=1)
            if index == 0:
                loads[part].wait()
            total += dot(hit, near[first:last])
        block = pl.ds(index * chunk, chunk)
        found[block] = total.astype(BF16).reshape((chunk, *found.shape[1:]))
        stores.append(
            pltpu.make_async_copy(found.at[block], pieces.at[block], written.at[index])
        )
        stores[-1].start()
    for store in stores:
        store.wait()


def offset_kernel(rows, codes, book, out):
    subs, width_sub, code_count = book.shape
    row_count = rows.shape[0]
    turned = codes[...].astype(F32).T.astype(I32)
    code_iota = lax.broadcasted_iota(I32, (row_count, code_count), 1)
    empty = jnp.zeros((width_sub, code_count), BF16)
    for pair in range(subs // 2):
        hits, highs, lows = [], [], []
        for m in (2 * pair, 2 * pair + 1):
            hits.append(mask_bf16(code_iota == turned[:, m : m + 1]))
            high = book[m].astype(BF16)
            highs.append(high)
            lows.append((book[m] - high.astype(F32)).astype(BF16))
        table = jnp.concatenate(
            [
                jnp.concatenate([highs[0], empty], axis=1),
                jnp.concatenate([empty, highs[1]], axis=1),
                jnp.concatenate([lows[0], empty], axis=1),
                jnp.concatenate([empty, lows[1]], axis=1),
            ],
            axis=0,
        )
        recon = dot_nt(jnp.concatenate(hits, axis=1), table)
        lanes = 2 * width_sub
        span = slice(pair * lanes, (pair + 1) * lanes)
        out[:, span] = rows[:, span].astype(F32) - (recon[:, :lanes] + recon[:, lanes:])


def error_kernel(valid, position, offsets, centres, out):
    slots, width = centres.shape
    row_count = offsets.shape[0]
    column_at = jnp.broadcast_to(position[...].astype(F32), (8, row_count)).T.astype(I32)[:, 0:1]
    hit = mask_bf16(lax.broadcasted_iota(I32, (row_count, slots), 1) == column_at)
    partial = jnp.zeros((row_count, 128), F32)
    for start in range(0, width, 256):
        gap = offsets[:, start : start + 256] - dot(hit, centres[:, start : start + 256])
        square = gap * gap
        partial += square[:, :128] + square[:, 128:]
    error = jnp.sum(partial.T, axis=0, keepdims=True) * (1.0 / width)
    lane = lax.broadcasted_iota(I32, (1, row_count), 1)
    out[...] = jnp.where(lane < valid[0], error, 0.0)


def scaled_codes(sums, counts, which):
    top = jnp.max(jnp.abs(sums), axis=0, keepdims=True)
    exponent = jnp.clip(jnp.ceil(jnp.log2(top)) - 1.0, -125.0, 127.0)
    scaled = jnp.clip(jnp.round(sums / jnp.exp2(exponent) * 16384.0), -32767.0, 32767.0)
    tail = jnp.where(which < 2, counts, jnp.where(which == 2, exponent, 0.0))
    return jnp.concatenate([scaled, tail], axis=0).astype(I32).astype(jnp.int16)


def add_kernel(width_sub, keep, got, own, *codes):
    replicas, half, padded, code_count = keep.shape
    which = lax.broadcasted_iota(I32, (padded - width_sub, code_count), 0)
    for step in range(replicas):
        for m in range(half):
            sums = keep[step, m, 0:width_sub] + got[step, m, 0:width_sub]
            counts = keep[step, m, width_sub:padded] + got[step, m, width_sub:padded]
            high = jnp.floor(counts * (1.0 / 256.0))
            counts = jnp.where(which == 0, high, counts - 256.0 * high)
            if step == 0:
                own[m, 0:width_sub] = sums
                own[m, width_sub:padded] = counts
            else:
                codes[step - 1][m] = scaled_codes(sums, counts, which)


def encode_kernel(width_sub, book, own, *refs):
    parts = refs[:-3]
    out, near, loaded = refs[-3:]
    half, padded, code_count = out.shape
    me, rep = lax.axis_index("list"), lax.axis_index("rep")
    start = (2 * rep + jnp.bitwise_and(me, 1)) * half
    load = pltpu.make_async_copy(book.at[pl.ds(start, half)], near, loaded)
    load.start()
    prior = jnp.where(me < 2, prior_weight, 0.0)
    which = lax.broadcasted_iota(I32, (padded - width_sub, code_count), 0)
    load.wait()
    for m in range(half):
        sums = own[m, 0:width_sub] + prior * near[m]
        counts = own[m, width_sub:padded] + jnp.where(which == 1, prior, 0.0)
        for part in parts:
            coded = part[m].astype(I32).astype(F32)
            tail = coded[width_sub:padded]
            sums += coded[0:width_sub] * (jnp.exp2(tail[2:3]) * (1.0 / 16384.0))
            counts += tail
        out[m] = scaled_codes(sums, counts, which)


def swap(array, axis, step):
    count = lax.axis_size(axis)
    return lax.ppermute(array, axis, [(i, i ^ step) for i in range(count)])


def struct(*shape, dtype=F32):
    return jax.ShapeDtypeStruct(shape, dtype)


def params(mib):
    return pltpu.CompilerParams(vmem_limit_bytes=mib << 20)


def cost(flops, size):
    return pl.CostEstimate(flops=int(flops), bytes_accessed=int(size), transcendentals=0)


def body(memory_rows, list_owner, list_slot, pq_codes, valid_rows, centroids, codebook):
    row_count, width = memory_rows.shape
    lists = centroids.shape[0]
    subs, code_count, width_sub = codebook.shape
    owners, replicas = lax.axis_size("list"), lax.axis_size("rep")
    capacity = max(128, 4 * row_count // owners)
    group_subs = subs // replicas
    half = group_subs // 2
    padded = width_sub + 8
    book = jnp.transpose(codebook, (0, 2, 1))
    codes = pq_codes.T

    requests, position = pl.pallas_call(
        functools.partial(pack_kernel, owners, capacity),
        in_specs=[SMEM] + [VMEM] * 3,
        out_specs=[VMEM] * 2,
        out_shape=[
            struct(owners, subs + extra, capacity, dtype=BF16),
            struct(1, row_count, dtype=I32),
        ],
        compiler_params=params(60),
        cost_estimate=cost(1000, 1000),
        name="pack",
    )(
        valid_rows,
        list_owner.reshape(1, row_count),
        list_slot.reshape(1, row_count),
        codes,
    )
    requests = lax.all_to_all(requests, "list", 0, 0, tiled=True)

    far, far_rows, far_codes = (
        pltpu.with_memory_space_constraint(array, pltpu.HBM)
        for array in (centroids, memory_rows, codes)
    )
    row_sums, held = pl.pallas_call(
        row_sums_kernel,
        in_specs=[SMEM] + [VMEM] * 2 + [HBM],
        out_specs=[VMEM] * 2,
        out_shape=[
            struct(subs, padded, code_count),
            struct(lists // 2, width, dtype=BF16),
        ],
        scratch_shapes=[pltpu.SemaphoreType.DMA],
        compiler_params=params(24),
        cost_estimate=cost(2 << 30, 4 << 20),
        name="row_sums",
    )(valid_rows, far_rows, far_codes, far)
    offsets = pl.pallas_call(
        offset_kernel,
        in_specs=[VMEM] * 3,
        out_specs=VMEM,
        out_shape=struct(row_count, width),
        compiler_params=params(48),
        cost_estimate=cost(1000, 1000),
        name="offsets",
    )(memory_rows, codes, book)
    gathered = pl.pallas_call(
        functools.partial(gather_kernel, subs),
        in_specs=[VMEM, VMEM, HBM],
        out_specs=HBM,
        out_shape=pltpu.HBM((owners, capacity, width), BF16),
        scratch_shapes=[
            pltpu.VMEM((lists - lists // 2, width), BF16),
            pltpu.VMEM((owners, capacity, width), BF16),
            pltpu.SemaphoreType.DMA((2,)),
            pltpu.SemaphoreType.DMA((4,)),
        ],
        compiler_params=params(20 + 5 * (owners * capacity * width >> 19)),
        cost_estimate=cost(4 << 30, 6 << 20),
        name="gather",
    )(requests, held, far)
    pieces = lax.all_to_all(gathered, "list", 0, 0, tiled=True)

    half_shape = struct(replicas, half, padded, code_count)
    keep, send = pl.pallas_call(
        functools.partial(sums_kernel, replicas),
        in_specs=[VMEM] * 3,
        out_specs=[VMEM] * 2,
        out_shape=[half_shape] * 2,
        compiler_params=params(20),
        cost_estimate=cost(1000, 1000),
        name="sums",
    )(requests, gathered.reshape(owners * capacity, width), row_sums)

    part_shape = (half, padded, code_count)
    own, *codes_out = pl.pallas_call(
        functools.partial(add_kernel, width_sub),
        in_specs=[VMEM] * 2,
        out_specs=[VMEM] * replicas,
        out_shape=[struct(*part_shape)]
        + [struct(*part_shape, dtype=jnp.int16)] * (replicas - 1),
        compiler_params=params(20),
        cost_estimate=cost(1000, 1000),
        name="add",
    )(keep, swap(send, "list", 1))
    parts = [own] + [swap(codes_out[s - 1], "rep", s) for s in range(1, replicas)]
    own = pl.pallas_call(
        functools.partial(encode_kernel, width_sub),
        in_specs=[HBM] + [VMEM] * replicas,
        out_specs=VMEM,
        out_shape=struct(half, padded, code_count, dtype=jnp.int16),
        scratch_shapes=[
            pltpu.VMEM((half, width_sub, code_count), F32),
            pltpu.SemaphoreType.DMA,
        ],
        compiler_params=params(20),
        cost_estimate=cost(1000, 1000),
        name="encode",
    )(book, *parts)
    own, offsets = lax.optimization_barrier((own, offsets))
    others = [swap(own, "list", s) for s in range(2, owners, 2)]
    row_error = pl.pallas_call(
        error_kernel,
        in_specs=[SMEM] + [VMEM] * 3,
        out_specs=VMEM,
        out_shape=struct(1, row_count),
        compiler_params=params(48),
        cost_estimate=cost(1000, 1000),
        name="errors",
    )(valid_rows, position, offsets, pieces.reshape(owners * capacity, width))
    row_error, *others = lax.optimization_barrier((row_error, *others))
    core = lax.axis_index("list") % 2
    parts = [part.astype(F32) for part in (own, *others)]
    parts = [
        jnp.where(
            lax.broadcasted_iota(I32, part.shape, 1) < width_sub,
            part * (jnp.exp2(part[:, width_sub + 2 : width_sub + 3]) / 16384.0),
            part,
        )
        for part in parts
    ]
    sums, high, low = (
        functools.reduce(jnp.add, [part[:, first:last] for part in parts])
        for first, last in (
            (0, width_sub),
            (width_sub, width_sub + 1),
            (width_sub + 1, width_sub + 2),
        )
    )
    own = sums / (256.0 * high + low)
    other = swap(own, "list", 1)
    new_codebook = jnp.concatenate(
        [jnp.where(core == 0, own, other), jnp.where(core == 0, other, own)], axis=0
    )
    return (jnp.transpose(new_codebook, (0, 2, 1)), row_error.reshape(row_count))


def solution(mesh):
    in_specs = (
        P(("list", "rep"), None),
        P(("list", "rep"), None),
        P(("list", "rep")),
        P(("list", "rep"), None),
        P(("list", "rep")),
        P("list", None),
        P(),
    )
    out_specs = (P("rep", None, None), P(("list", "rep")))
    return jax.shard_map(body, mesh=mesh, in_specs=in_specs, out_specs=out_specs, check_vma=False)
```

```python
import functools

import jax
import jax.numpy as jnp
from jax import lax
from jax.experimental import pallas as pl
from jax.experimental.pallas import tpu as pltpu
from jax.sharding import PartitionSpec as P

prior_weight = 4.0
F32, BF16, I32 = jnp.float32, jnp.bfloat16, jnp.int32
VMEM = pl.BlockSpec(memory_space=pltpu.VMEM)
HBM = pl.BlockSpec(memory_space=pltpu.HBM)
SMEM = pl.BlockSpec(memory_space=pltpu.SMEM)
NT = (((1,), (1,)), ((), ()))
extra = 16


def mask_bf16(mask):
    return jnp.where(mask, 1.0, 0.0).astype(BF16)


def dot(a, b):
    return jnp.dot(a, b, preferred_element_type=F32)


def dot_nt(a, b):
    return lax.dot_general(a, b, NT, preferred_element_type=F32)


def pack_kernel(owners, capacity, valid, owner, slot, codes, requests, position_out):
    row_count = owner.shape[1]
    lane = lax.broadcasted_iota(I32, (1, row_count), 1)
    live = lane < valid[0]
    target = jnp.where(live, owner[...], -1)
    hit = jnp.where(lax.broadcasted_iota(I32, (owners, row_count), 0) == target, 1.0, 0.0)
    earlier = mask_bf16(
        lax.broadcasted_iota(I32, (row_count, row_count), 0)
        < lax.broadcasted_iota(I32, (row_count, row_count), 1)
    )
    before = dot(hit.astype(BF16), earlier)
    rank = jnp.sum(hit * before, axis=0, keepdims=True).astype(I32)
    position = jnp.where(live, target * capacity + rank, -1)
    position_out[...] = position

    high = (slot[...] // 256).astype(F32)
    low = (slot[...] % 256).astype(F32)
    which = lax.broadcasted_iota(I32, (extra, row_count), 0)
    tail = jnp.where(which == 0, high, jnp.where(which == 1, low, 0.0))
    info = jnp.concatenate([codes[...].astype(F32) - 256.0, tail], axis=0).astype(BF16)
    within = lax.broadcasted_iota(I32, (capacity, row_count), 0)
    for dest in range(owners):
        place_at = mask_bf16(within == position - dest * capacity)
        requests[dest] = dot_nt(info, place_at).astype(BF16)


def row_sums_kernel(valid, rows, codes, centres, out, held, loaded):
    load = pltpu.make_async_copy(centres.at[pl.ds(0, held.shape[0])], held, loaded)
    load.start()
    subs, padded, code_count = out.shape
    row_count, width = rows.shape
    width_sub = width // subs
    lane = lax.broadcasted_iota(I32, (1, row_count), 1)
    live_codes = jnp.where(lane < valid[0], codes[...], -1)
    columns = rows[...].T
    code_iota = lax.broadcasted_iota(I32, (code_count, row_count), 0)
    ones = jnp.ones((16, row_count), BF16)
    for m in range(subs):
        code_hit = mask_bf16(code_iota == live_codes[m : m + 1])
        part = jnp.concatenate([columns[m * width_sub : (m + 1) * width_sub], ones], axis=0)
        out[m] = dot_nt(part, code_hit)[0:padded]
    load.wait()


def sums_kernel(replicas, requests, gathered, row_sums, keep, send):
    subs, padded, code_count = row_sums.shape
    owners, _, capacity = requests.shape
    slots, width = gathered.shape
    width_sub = width // subs
    group_subs = subs // replicas
    half = group_subs // 2
    mine = jnp.bitwise_and(lax.axis_index("list"), 1)
    rep = lax.axis_index("rep")
    asked = jnp.concatenate([requests[j] for j in range(owners)], axis=1)
    codes = asked.astype(F32).astype(I32) + 256
    code_iota = lax.broadcasted_iota(I32, (code_count, slots), 0)
    first = lax.broadcasted_iota(I32, (code_count, 2 * width_sub), 1) < width_sub
    for pair in range(subs // 2):
        span = slice(pair * 2 * width_sub, (pair + 1) * 2 * width_sub)
        found = [
            dot(mask_bf16(code_iota == codes[m : m + 1]), gathered[:, span])
            for m in (2 * pair, 2 * pair + 1)
        ]
        centre_sums = jnp.where(first, found[0], found[1]).T
        for j in range(2):
            m = 2 * pair + j
            sums = row_sums[m, 0:width_sub] - centre_sums[j * width_sub : (j + 1) * width_sub]
            counts = row_sums[m, width_sub:padded]
            group, at = m // group_subs, m % group_subs
            step = jnp.bitwise_xor(rep, group)

            def store(out, sums=sums, counts=counts, step=step, at=at):
                out[step, at % half, 0:width_sub] = sums
                out[step, at % half, width_sub:padded] = counts

            pl.when(mine == at // half)(functools.partial(store, keep))
            pl.when(mine != at // half)(functools.partial(store, send))


def gather_kernel(subs, requests, held, centres, pieces, near, found, loaded, written):
    owners, _, capacity = requests.shape
    lists = centres.shape[0]
    ready = held.shape[0]
    parts, chunks = loaded.shape[0], written.shape[0]
    chunk = owners // chunks
    span = chunk * capacity
    step = (lists - ready) // parts
    loads, stores = [], []
    for part in range(parts):
        load = pltpu.make_async_copy(
            centres.at[pl.ds(ready + part * step, step)],
            near.at[pl.ds(part * step, step)],
            loaded.at[part],
        )
        load.start()
        loads.append(load)
    for index in range(chunks):
        asked = jnp.concatenate([requests[index * chunk + j] for j in range(chunk)], axis=1)
        turned = asked.astype(F32).T.astype(I32)
        high, low = (turned[:, subs + i : subs + i + 1] for i in range(2))
        low_hit = mask_bf16(lax.broadcasted_iota(I32, (span, 256), 1) == low)
        hits = [low_hit * mask_bf16(high == h) for h in range(lists // 256)]
        total = dot(jnp.concatenate(hits[: ready // 256], axis=1), held[...])
        for part in range(parts):
            first, last = part * step, (part + 1) * step
            hit = jnp.concatenate(hits[(ready + first) // 256 : (ready + last) // 256], axis=1)
            if index == 0:
                loads[part].wait()
            total += dot(hit, near[first:last])
        block = pl.ds(index * chunk, chunk)
        found[block] = total.astype(BF16).reshape((chunk, *found.shape[1:]))
        stores.append(
            pltpu.make_async_copy(found.at[block], pieces.at[block], written.at[index])
        )
        stores[-1].start()
    for store in stores:
        store.wait()


def offset_kernel(rows, codes, book, out):
    subs, width_sub, code_count = book.shape
    row_count = rows.shape[0]
    turned = codes[...].astype(F32).T.astype(I32)
    code_iota = lax.broadcasted_iota(I32, (row_count, code_count), 1)
    empty = jnp.zeros((width_sub, code_count), BF16)
    for pair in range(subs // 2):
        hits, highs, lows = [], [], []
        for m in (2 * pair, 2 * pair + 1):
            hits.append(mask_bf16(code_iota == turned[:, m : m + 1]))
            high = book[m].astype(BF16)
            highs.append(high)
            lows.append((book[m] - high.astype(F32)).astype(BF16))
        table = jnp.concatenate(
            [
                jnp.concatenate([highs[0], empty], axis=1),
                jnp.concatenate([empty, highs[1]], axis=1),
                jnp.concatenate([lows[0], empty], axis=1),
                jnp.concatenate([empty, lows[1]], axis=1),
            ],
            axis=0,
        )
        recon = dot_nt(jnp.concatenate(hits, axis=1), table)
        lanes = 2 * width_sub
        span = slice(pair * lanes, (pair + 1) * lanes)
        out[:, span] = rows[:, span].astype(F32) - (recon[:, :lanes] + recon[:, lanes:])


def error_kernel(valid, position, offsets, centres, out):
    slots, width = centres.shape
    row_count = offsets.shape[0]
    column_at = jnp.broadcast_to(position[...].astype(F32), (8, row_count)).T.astype(I32)[:, 0:1]
    hit = mask_bf16(lax.broadcasted_iota(I32, (row_count, slots), 1) == column_at)
    partial = jnp.zeros((row_count, 128), F32)
    for start in range(0, width, 256):
        gap = offsets[:, start : start + 256] - dot(hit, centres[:, start : start + 256])
        square = gap * gap
        partial += square[:, :128] + square[:, 128:]
    error = jnp.sum(partial.T, axis=0, keepdims=True) * (1.0 / width)
    lane = lax.broadcasted_iota(I32, (1, row_count), 1)
    out[...] = jnp.where(lane < valid[0], error, 0.0)


def scaled_codes(sums, counts, which):
    top = jnp.max(jnp.abs(sums), axis=0, keepdims=True)
    exponent = jnp.clip(jnp.ceil(jnp.log2(top)) - 1.0, -125.0, 127.0)
    scaled = jnp.clip(jnp.round(sums / jnp.exp2(exponent) * 16384.0), -32767.0, 32767.0)
    tail = jnp.where(which < 2, counts, jnp.where(which == 2, exponent, 0.0))
    return jnp.concatenate([scaled, tail], axis=0).astype(I32).astype(jnp.int16)


def add_kernel(width_sub, keep, got, own, *codes):
    replicas, half, padded, code_count = keep.shape
    which = lax.broadcasted_iota(I32, (padded - width_sub, code_count), 0)
    for step in range(replicas):
        for m in range(half):
            sums = keep[step, m, 0:width_sub] + got[step, m, 0:width_sub]
            counts = keep[step, m, width_sub:padded] + got[step, m, width_sub:padded]
            high = jnp.floor(counts * (1.0 / 256.0))
            counts = jnp.where(which == 0, high, counts - 256.0 * high)
            if step == 0:
                own[m, 0:width_sub] = sums
                own[m, width_sub:padded] = counts
            else:
                codes[step - 1][m] = scaled_codes(sums, counts, which)


def encode_kernel(width_sub, book, own, *refs):
    parts = refs[:-3]
    out, near, loaded = refs[-3:]
    half, padded, code_count = out.shape
    me, rep = lax.axis_index("list"), lax.axis_index("rep")
    start = (2 * rep + jnp.bitwise_and(me, 1)) * half
    load = pltpu.make_async_copy(book.at[pl.ds(start, half)], near, loaded)
    load.start()
    prior = jnp.where(me < 2, prior_weight, 0.0)
    which = lax.broadcasted_iota(I32, (padded - width_sub, code_count), 0)
    load.wait()
    for m in range(half):
        sums = own[m, 0:width_sub] + prior * near[m]
        counts = own[m, width_sub:padded] + jnp.where(which == 1, prior, 0.0)
        for part in parts:
            coded = part[m].astype(I32).astype(F32)
            tail = coded[width_sub:padded]
            sums += coded[0:width_sub] * (jnp.exp2(tail[2:3]) * (1.0 / 16384.0))
            counts += tail
        out[m] = scaled_codes(sums, counts, which)


def finish_kernel(width_sub, *refs):
    parts, out = refs[:-1], refs[-1]
    for m in range(out.shape[0]):
        coded = [part[m].astype(I32).astype(F32) for part in parts]
        sums = sum(
            code[0:width_sub] * (jnp.exp2(code[width_sub + 2 : width_sub + 3]) * (1.0 / 16384.0))
            for code in coded
        )
        high, low = (
            sum(code[width_sub + i : width_sub + i + 1] for code in coded) for i in range(2)
        )
        out[m] = sums / (256.0 * high + low)


def swap(array, axis, step):
    count = lax.axis_size(axis)
    return lax.ppermute(array, axis, [(i, i ^ step) for i in range(count)])


def struct(*shape, dtype=F32):
    return jax.ShapeDtypeStruct(shape, dtype)


def params(mib):
    return pltpu.CompilerParams(vmem_limit_bytes=mib << 20)


def cost(flops, size):
    return pl.CostEstimate(flops=int(flops), bytes_accessed=int(size), transcendentals=0)


def body(memory_rows, list_owner, list_slot, pq_codes, valid_rows, centroids, codebook):
    row_count, width = memory_rows.shape
    lists = centroids.shape[0]
    subs, code_count, width_sub = codebook.shape
    owners, replicas = lax.axis_size("list"), lax.axis_size("rep")
    capacity = max(128, 4 * row_count // owners)
    group_subs = subs // replicas
    half = group_subs // 2
    padded = width_sub + 8
    book = jnp.transpose(codebook, (0, 2, 1))
    codes = pq_codes.T

    requests, position = pl.pallas_call(
        functools.partial(pack_kernel, owners, capacity),
        in_specs=[SMEM] + [VMEM] * 3,
        out_specs=[VMEM] * 2,
        out_shape=[
            struct(owners, subs + extra, capacity, dtype=BF16),
            struct(1, row_count, dtype=I32),
        ],
        compiler_params=params(60),
        cost_estimate=cost(1000, 1000),
        name="pack",
    )(
        valid_rows,
        list_owner.reshape(1, row_count),
        list_slot.reshape(1, row_count),
        codes,
    )
    requests = lax.all_to_all(requests, "list", 0, 0, tiled=True)

    far, far_rows, far_codes = (
        pltpu.with_memory_space_constraint(array, pltpu.HBM)
        for array in (centroids, memory_rows, codes)
    )
    row_sums, held = pl.pallas_call(
        row_sums_kernel,
        in_specs=[SMEM] + [VMEM] * 2 + [HBM],
        out_specs=[VMEM] * 2,
        out_shape=[
            struct(subs, padded, code_count),
            struct(lists // 2, width, dtype=BF16),
        ],
        scratch_shapes=[pltpu.SemaphoreType.DMA],
        compiler_params=params(24),
        cost_estimate=cost(2 << 30, 4 << 20),
        name="row_sums",
    )(valid_rows, far_rows, far_codes, far)
    offsets = pl.pallas_call(
        offset_kernel,
        in_specs=[VMEM] * 3,
        out_specs=VMEM,
        out_shape=struct(row_count, width),
        compiler_params=params(48),
        cost_estimate=cost(1000, 1000),
        name="offsets",
    )(memory_rows, codes, book)
    gathered = pl.pallas_call(
        functools.partial(gather_kernel, subs),
        in_specs=[VMEM, VMEM, HBM],
        out_specs=HBM,
        out_shape=pltpu.HBM((owners, capacity, width), BF16),
        scratch_shapes=[
            pltpu.VMEM((lists - lists // 2, width), BF16),
            pltpu.VMEM((owners, capacity, width), BF16),
            pltpu.SemaphoreType.DMA((2,)),
            pltpu.SemaphoreType.DMA((4,)),
        ],
        compiler_params=params(20 + 5 * (owners * capacity * width >> 19)),
        cost_estimate=cost(4 << 30, 6 << 20),
        name="gather",
    )(requests, held, far)
    pieces = lax.all_to_all(gathered, "list", 0, 0, tiled=True)

    half_shape = struct(replicas, half, padded, code_count)
    keep, send = pl.pallas_call(
        functools.partial(sums_kernel, replicas),
        in_specs=[VMEM] * 3,
        out_specs=[VMEM] * 2,
        out_shape=[half_shape] * 2,
        compiler_params=params(20),
        cost_estimate=cost(1000, 1000),
        name="sums",
    )(requests, gathered.reshape(owners * capacity, width), row_sums)

    part_shape = (half, padded, code_count)
    own, *codes_out = pl.pallas_call(
        functools.partial(add_kernel, width_sub),
        in_specs=[VMEM] * 2,
        out_specs=[VMEM] * replicas,
        out_shape=[struct(*part_shape)]
        + [struct(*part_shape, dtype=jnp.int16)] * (replicas - 1),
        compiler_params=params(20),
        cost_estimate=cost(1000, 1000),
        name="add",
    )(keep, swap(send, "list", 1))
    parts = [own] + [swap(codes_out[s - 1], "rep", s) for s in range(1, replicas)]
    own = pl.pallas_call(
        functools.partial(encode_kernel, width_sub),
        in_specs=[HBM] + [VMEM] * replicas,
        out_specs=VMEM,
        out_shape=struct(half, padded, code_count, dtype=jnp.int16),
        scratch_shapes=[
            pltpu.VMEM((half, width_sub, code_count), F32),
            pltpu.SemaphoreType.DMA,
        ],
        compiler_params=params(20),
        cost_estimate=cost(1000, 1000),
        name="encode",
    )(book, *parts)
    own, offsets = lax.optimization_barrier((own, offsets))
    others = [swap(own, "list", s) for s in range(2, owners, 2)]
    row_error = pl.pallas_call(
        error_kernel,
        in_specs=[SMEM] + [VMEM] * 3,
        out_specs=VMEM,
        out_shape=struct(1, row_count),
        compiler_params=params(48),
        cost_estimate=cost(1000, 1000),
        name="errors",
    )(valid_rows, position, offsets, pieces.reshape(owners * capacity, width))
    row_error, *others = lax.optimization_barrier((row_error, *others))
    core = lax.axis_index("list") % 2
    own = pl.pallas_call(
        functools.partial(finish_kernel, width_sub),
        in_specs=[VMEM] * (1 + len(others)),
        out_specs=VMEM,
        out_shape=struct(half, width_sub, code_count),
        compiler_params=params(20),
        cost_estimate=cost(1000, 1000),
        name="finish",
    )(own, *others)
    other = swap(own, "list", 1)
    new_codebook = jnp.concatenate(
        [jnp.where(core == 0, own, other), jnp.where(core == 0, other, own)], axis=0
    )
    return (jnp.transpose(new_codebook, (0, 2, 1)), row_error.reshape(row_count))


def solution(mesh):
    in_specs = (
        P(("list", "rep"), None),
        P(("list", "rep"), None),
        P(("list", "rep")),
        P(("list", "rep"), None),
        P(("list", "rep")),
        P("list", None),
        P(),
    )
    out_specs = (P("rep", None, None), P(("list", "rep")))
    return jax.shard_map(body, mesh=mesh, in_specs=in_specs, out_specs=out_specs, check_vma=False)
```

```python
import functools

import jax
import jax.numpy as jnp
from jax import lax
from jax.experimental import pallas as pl
from jax.experimental.pallas import tpu as pltpu
from jax.sharding import PartitionSpec as P

prior_weight = 4.0
F32, BF16, I32 = jnp.float32, jnp.bfloat16, jnp.int32
VMEM = pl.BlockSpec(memory_space=pltpu.VMEM)
HBM = pl.BlockSpec(memory_space=pltpu.HBM)
SMEM = pl.BlockSpec(memory_space=pltpu.SMEM)
NT = (((1,), (1,)), ((), ()))
extra = 16


def mask_bf16(mask):
    return jnp.where(mask, 1.0, 0.0).astype(BF16)


def dot(a, b):
    return jnp.dot(a, b, preferred_element_type=F32)


def dot_nt(a, b):
    return lax.dot_general(a, b, NT, preferred_element_type=F32)


def pack_kernel(owners, capacity, valid, owner, slot, codes, requests, position_out):
    row_count = owner.shape[1]
    lane = lax.broadcasted_iota(I32, (1, row_count), 1)
    live = lane < valid[0]
    target = jnp.where(live, owner[...], -1)
    hit = jnp.where(lax.broadcasted_iota(I32, (owners, row_count), 0) == target, 1.0, 0.0)
    earlier = mask_bf16(
        lax.broadcasted_iota(I32, (row_count, row_count), 0)
        < lax.broadcasted_iota(I32, (row_count, row_count), 1)
    )
    before = dot(hit.astype(BF16), earlier)
    rank = jnp.sum(hit * before, axis=0, keepdims=True).astype(I32)
    position = jnp.where(live, target * capacity + rank, -1)
    position_out[...] = position

    high = (slot[...] // 256).astype(F32)
    low = (slot[...] % 256).astype(F32)
    which = lax.broadcasted_iota(I32, (extra, row_count), 0)
    tail = jnp.where(which == 0, high, jnp.where(which == 1, low, 0.0))
    info = jnp.concatenate([codes[...].astype(F32) - 256.0, tail], axis=0).astype(BF16)
    within = lax.broadcasted_iota(I32, (capacity, row_count), 0)
    for dest in range(owners):
        place_at = mask_bf16(within == position - dest * capacity)
        requests[dest] = dot_nt(info, place_at).astype(BF16)


def row_sums_kernel(valid, rows, codes, centres, out, held, loaded):
    load = pltpu.make_async_copy(centres.at[pl.ds(0, held.shape[0])], held, loaded)
    load.start()
    subs, padded, code_count = out.shape
    row_count, width = rows.shape
    width_sub = width // subs
    lane = lax.broadcasted_iota(I32, (1, row_count), 1)
    live_codes = jnp.where(lane < valid[0], codes[...], -1)
    columns = rows[...].T
    code_iota = lax.broadcasted_iota(I32, (code_count, row_count), 0)
    ones = jnp.ones((16, row_count), BF16)
    for m in range(subs):
        code_hit = mask_bf16(code_iota == live_codes[m : m + 1])
        part = jnp.concatenate([columns[m * width_sub : (m + 1) * width_sub], ones], axis=0)
        out[m] = dot_nt(part, code_hit)[0:padded]
    load.wait()


def sums_kernel(replicas, requests, gathered, row_sums, keep, send):
    subs, padded, code_count = row_sums.shape
    owners, _, capacity = requests.shape
    slots, width = gathered.shape
    width_sub = width // subs
    group_subs = subs // replicas
    half = group_subs // 2
    mine = jnp.bitwise_and(lax.axis_index("list"), 1)
    rep = lax.axis_index("rep")
    asked = jnp.concatenate([requests[j] for j in range(owners)], axis=1)
    codes = asked.astype(F32).astype(I32) + 256
    code_iota = lax.broadcasted_iota(I32, (code_count, slots), 0)
    first = lax.broadcasted_iota(I32, (code_count, 2 * width_sub), 1) < width_sub
    for pair in range(subs // 2):
        span = slice(pair * 2 * width_sub, (pair + 1) * 2 * width_sub)
        found = [
            dot(mask_bf16(code_iota == codes[m : m + 1]), gathered[:, span])
            for m in (2 * pair, 2 * pair + 1)
        ]
        centre_sums = jnp.where(first, found[0], found[1]).T
        for j in range(2):
            m = 2 * pair + j
            sums = row_sums[m, 0:width_sub] - centre_sums[j * width_sub : (j + 1) * width_sub]
            counts = row_sums[m, width_sub:padded]
            group, at = m // group_subs, m % group_subs
            step = jnp.bitwise_xor(rep, group)

            def store(out, sums=sums, counts=counts, step=step, at=at):
                out[step, at % half, 0:width_sub] = sums
                out[step, at % half, width_sub:padded] = counts

            pl.when(mine == at // half)(functools.partial(store, keep))
            pl.when(mine != at // half)(functools.partial(store, send))


def gather_kernel(subs, requests, held, centres, pieces, near, found, loaded, written):
    owners, _, capacity = requests.shape
    lists = centres.shape[0]
    ready = held.shape[0]
    parts, chunks = loaded.shape[0], written.shape[0]
    chunk = owners // chunks
    span = chunk * capacity
    step = (lists - ready) // parts
    loads, stores = [], []
    for part in range(parts):
        load = pltpu.make_async_copy(
            centres.at[pl.ds(ready + part * step, step)],
            near.at[pl.ds(part * step, step)],
            loaded.at[part],
        )
        load.start()
        loads.append(load)
    for index in range(chunks):
        asked = jnp.concatenate([requests[index * chunk + j] for j in range(chunk)], axis=1)
        turned = asked.astype(F32).T.astype(I32)
        high, low = (turned[:, subs + i : subs + i + 1] for i in range(2))
        low_hit = mask_bf16(lax.broadcasted_iota(I32, (span, 256), 1) == low)
        hits = [low_hit * mask_bf16(high == h) for h in range(lists // 256)]
        total = dot(jnp.concatenate(hits[: ready // 256], axis=1), held[...])
        for part in range(parts):
            first, last = part * step, (part + 1) * step
            hit = jnp.concatenate(hits[(ready + first) // 256 : (ready + last) // 256], axis=1)
            if index == 0:
                loads[part].wait()
            total += dot(hit, near[first:last])
        block = pl.ds(index * chunk, chunk)
        found[block] = total.astype(BF16).reshape((chunk, *found.shape[1:]))
        stores.append(
            pltpu.make_async_copy(found.at[block], pieces.at[block], written.at[index])
        )
        stores[-1].start()
    for store in stores:
        store.wait()


def offset_kernel(rows, codes, book, out):
    subs, width_sub, code_count = book.shape
    row_count = rows.shape[0]
    turned = codes[...].astype(F32).T.astype(I32)
    code_iota = lax.broadcasted_iota(I32, (row_count, code_count), 1)
    empty = jnp.zeros((width_sub, code_count), BF16)
    for pair in range(subs // 2):
        hits, highs, lows = [], [], []
        for m in (2 * pair, 2 * pair + 1):
            hits.append(mask_bf16(code_iota == turned[:, m : m + 1]))
            high = book[m].astype(BF16)
            highs.append(high)
            lows.append((book[m] - high.astype(F32)).astype(BF16))
        table = jnp.concatenate(
            [
                jnp.concatenate([highs[0], empty], axis=1),
                jnp.concatenate([empty, highs[1]], axis=1),
                jnp.concatenate([lows[0], empty], axis=1),
                jnp.concatenate([empty, lows[1]], axis=1),
            ],
            axis=0,
        )
        recon = dot_nt(jnp.concatenate(hits, axis=1), table)
        lanes = 2 * width_sub
        span = slice(pair * lanes, (pair + 1) * lanes)
        out[:, span] = rows[:, span].astype(F32) - (recon[:, :lanes] + recon[:, lanes:])


def error_kernel(valid, position, offsets, centres, out):
    slots, width = centres.shape
    row_count = offsets.shape[0]
    column_at = jnp.broadcast_to(position[...].astype(F32), (8, row_count)).T.astype(I32)[:, 0:1]
    hit = mask_bf16(lax.broadcasted_iota(I32, (row_count, slots), 1) == column_at)
    partial = jnp.zeros((row_count, 128), F32)
    for start in range(0, width, 256):
        gap = offsets[:, start : start + 256] - dot(hit, centres[:, start : start + 256])
        square = gap * gap
        partial += square[:, :128] + square[:, 128:]
    error = jnp.sum(partial.T, axis=0, keepdims=True) * (1.0 / width)
    lane = lax.broadcasted_iota(I32, (1, row_count), 1)
    out[...] = jnp.where(lane < valid[0], error, 0.0)


def scaled_codes(sums, counts, which):
    top = jnp.max(jnp.abs(sums), axis=0, keepdims=True)
    exponent = jnp.clip(jnp.ceil(jnp.log2(top)) - 1.0, -125.0, 127.0)
    scaled = jnp.clip(jnp.round(sums / jnp.exp2(exponent) * 16384.0), -32767.0, 32767.0)
    tail = jnp.where(which < 2, counts, jnp.where(which == 2, exponent, 0.0))
    return jnp.concatenate([scaled, tail], axis=0).astype(I32).astype(jnp.int16)


def add_kernel(width_sub, keep, got, own, *codes):
    replicas, half, padded, code_count = keep.shape
    which = lax.broadcasted_iota(I32, (padded - width_sub, code_count), 0)
    for step in range(replicas):
        for m in range(half):
            sums = keep[step, m, 0:width_sub] + got[step, m, 0:width_sub]
            counts = keep[step, m, width_sub:padded] + got[step, m, width_sub:padded]
            high = jnp.floor(counts * (1.0 / 256.0))
            counts = jnp.where(which == 0, high, counts - 256.0 * high)
            if step == 0:
                own[m, 0:width_sub] = sums
                own[m, width_sub:padded] = counts
            else:
                codes[step - 1][m] = scaled_codes(sums, counts, which)


def encode_kernel(width_sub, book, own, *refs):
    parts = refs[:-3]
    out, near, loaded = refs[-3:]
    half, padded, code_count = out.shape
    me, rep = lax.axis_index("list"), lax.axis_index("rep")
    start = (2 * rep + jnp.bitwise_and(me, 1)) * half
    load = pltpu.make_async_copy(book.at[pl.ds(start, half)], near, loaded)
    load.start()
    prior = jnp.where(me < 2, prior_weight, 0.0)
    which = lax.broadcasted_iota(I32, (padded - width_sub, code_count), 0)
    load.wait()
    for m in range(half):
        sums = own[m, 0:width_sub] + prior * near[m]
        counts = own[m, width_sub:padded] + jnp.where(which == 1, prior, 0.0)
        for part in parts:
            coded = part[m].astype(I32).astype(F32)
            tail = coded[width_sub:padded]
            sums += coded[0:width_sub] * (jnp.exp2(tail[2:3]) * (1.0 / 16384.0))
            counts += tail
        out[m] = scaled_codes(sums, counts, which)


def finish_kernel(width_sub, *refs):
    parts, out = refs[:-1], refs[-1]
    for m in range(out.shape[0]):
        coded = [part[m].astype(I32).astype(F32) for part in parts]
        sums = sum(
            code[0:width_sub] * (jnp.exp2(code[width_sub + 2 : width_sub + 3]) * (1.0 / 16384.0))
            for code in coded
        )
        high, low = (
            sum(code[width_sub + i : width_sub + i + 1] for code in coded) for i in range(2)
        )
        out[m] = sums / (256.0 * high + low)


def swap(array, axis, step):
    count = lax.axis_size(axis)
    return lax.ppermute(array, axis, [(i, i ^ step) for i in range(count)])


def struct(*shape, dtype=F32):
    return jax.ShapeDtypeStruct(shape, dtype)


def params(mib):
    return pltpu.CompilerParams(vmem_limit_bytes=mib << 20)


def cost(flops, size):
    return pl.CostEstimate(flops=int(flops), bytes_accessed=int(size), transcendentals=0)


def body(memory_rows, list_owner, list_slot, pq_codes, valid_rows, centroids, codebook):
    row_count, width = memory_rows.shape
    lists = centroids.shape[0]
    subs, code_count, width_sub = codebook.shape
    owners, replicas = lax.axis_size("list"), lax.axis_size("rep")
    capacity = max(128, 4 * row_count // owners)
    group_subs = subs // replicas
    half = group_subs // 2
    padded = width_sub + 8
    book = jnp.transpose(codebook, (0, 2, 1))
    codes = pq_codes.T

    requests, position = pl.pallas_call(
        functools.partial(pack_kernel, owners, capacity),
        in_specs=[SMEM] + [VMEM] * 3,
        out_specs=[VMEM] * 2,
        out_shape=[
            struct(owners, subs + extra, capacity, dtype=BF16),
            struct(1, row_count, dtype=I32),
        ],
        compiler_params=params(60),
        cost_estimate=cost(1000, 1000),
        name="pack",
    )(
        valid_rows,
        list_owner.reshape(1, row_count),
        list_slot.reshape(1, row_count),
        codes,
    )
    requests = lax.all_to_all(requests, "list", 0, 0, tiled=True)

    far, far_rows, far_codes = (
        pltpu.with_memory_space_constraint(array, pltpu.HBM)
        for array in (centroids, memory_rows, codes)
    )
    row_sums, held = pl.pallas_call(
        row_sums_kernel,
        in_specs=[SMEM] + [VMEM] * 2 + [HBM],
        out_specs=[VMEM] * 2,
        out_shape=[
            struct(subs, padded, code_count),
            struct(lists // 2, width, dtype=BF16),
        ],
        scratch_shapes=[pltpu.SemaphoreType.DMA],
        compiler_params=params(24),
        cost_estimate=cost(2 << 30, 4 << 20),
        name="row_sums",
    )(valid_rows, far_rows, far_codes, far)
    offsets = pl.pallas_call(
        offset_kernel,
        in_specs=[VMEM] * 3,
        out_specs=VMEM,
        out_shape=struct(row_count, width),
        compiler_params=params(48),
        cost_estimate=cost(1 << 30, 2 << 20),
        name="offsets",
    )(memory_rows, codes, book)
    gathered = pl.pallas_call(
        functools.partial(gather_kernel, subs),
        in_specs=[VMEM, VMEM, HBM],
        out_specs=HBM,
        out_shape=pltpu.HBM((owners, capacity, width), BF16),
        scratch_shapes=[
            pltpu.VMEM((lists - lists // 2, width), BF16),
            pltpu.VMEM((owners, capacity, width), BF16),
            pltpu.SemaphoreType.DMA((2,)),
            pltpu.SemaphoreType.DMA((4,)),
        ],
        compiler_params=params(20 + 5 * (owners * capacity * width >> 19)),
        cost_estimate=cost(4 << 30, 6 << 20),
        name="gather",
    )(requests, held, far)
    pieces = lax.all_to_all(gathered, "list", 0, 0, tiled=True)

    half_shape = struct(replicas, half, padded, code_count)
    keep, send = pl.pallas_call(
        functools.partial(sums_kernel, replicas),
        in_specs=[VMEM] * 3,
        out_specs=[VMEM] * 2,
        out_shape=[half_shape] * 2,
        compiler_params=params(20),
        cost_estimate=cost(4 << 30, 4 << 20),
        name="sums",
    )(requests, gathered.reshape(owners * capacity, width), row_sums)

    part_shape = (half, padded, code_count)
    own, *codes_out = pl.pallas_call(
        functools.partial(add_kernel, width_sub),
        in_specs=[VMEM] * 2,
        out_specs=[VMEM] * replicas,
        out_shape=[struct(*part_shape)]
        + [struct(*part_shape, dtype=jnp.int16)] * (replicas - 1),
        compiler_params=params(20),
        cost_estimate=cost(1000, 1000),
        name="add",
    )(keep, swap(send, "list", 1))
    parts = [own] + [swap(codes_out[s - 1], "rep", s) for s in range(1, replicas)]
    own = pl.pallas_call(
        functools.partial(encode_kernel, width_sub),
        in_specs=[HBM] + [VMEM] * replicas,
        out_specs=VMEM,
        out_shape=struct(half, padded, code_count, dtype=jnp.int16),
        scratch_shapes=[
            pltpu.VMEM((half, width_sub, code_count), F32),
            pltpu.SemaphoreType.DMA,
        ],
        compiler_params=params(20),
        cost_estimate=cost(1000, 1000),
        name="encode",
    )(book, *parts)
    own, offsets = lax.optimization_barrier((own, offsets))
    others = [swap(own, "list", s) for s in range(2, owners, 2)]
    row_error = pl.pallas_call(
        error_kernel,
        in_specs=[SMEM] + [VMEM] * 3,
        out_specs=VMEM,
        out_shape=struct(1, row_count),
        compiler_params=params(48),
        cost_estimate=cost(1000, 1000),
        name="errors",
    )(valid_rows, position, offsets, pieces.reshape(owners * capacity, width))
    row_error, *others = lax.optimization_barrier((row_error, *others))
    core = lax.axis_index("list") % 2
    own = pl.pallas_call(
        functools.partial(finish_kernel, width_sub),
        in_specs=[VMEM] * (1 + len(others)),
        out_specs=VMEM,
        out_shape=struct(half, width_sub, code_count),
        compiler_params=params(20),
        cost_estimate=cost(1000, 1000),
        name="finish",
    )(own, *others)
    other = swap(own, "list", 1)
    new_codebook = jnp.concatenate(
        [jnp.where(core == 0, own, other), jnp.where(core == 0, other, own)], axis=0
    )
    return (jnp.transpose(new_codebook, (0, 2, 1)), row_error.reshape(row_count))


def solution(mesh):
    in_specs = (
        P(("list", "rep"), None),
        P(("list", "rep"), None),
        P(("list", "rep")),
        P(("list", "rep"), None),
        P(("list", "rep")),
        P("list", None),
        P(),
    )
    out_specs = (P("rep", None, None), P(("list", "rep")))
    return jax.shard_map(body, mesh=mesh, in_specs=in_specs, out_specs=out_specs, check_vma=False)
```
